128 devices in a mesh: gx: 4 (over z), gy: 4 (over x), gz: 8 (over y, core).
Axes of the slice: x: 4, y: 4, z: 4, core: 2. Of those that a mesh axis runs over, the one named last changes fastest.
Arguments:
- stencil: bfloat16 [7, 4, 32, 128, 2048], P(None, None, 'gx', 'gy', 'gz'), may hold values from -1.5 to 13, as said below
- right_side: float32 [2, 32, 128, 2048], P(None, 'gx', 'gy', 'gz'), may hold values from -25 to 25
Outputs:
- solution: float32 [2, 32, 128, 2048], P(None, 'gx', 'gy', 'gz')
- residual: float32 [2, 32, 128, 2048], P(None, 'gx', 'gy', 'gz')
The draws below stay inside these ranges and needn't reach their ends.
Inputs may be any that keep to these rules, and one draw needn't show every extreme that they name: `stencil`: entries of the operator's blocks.
All inputs are finite; a program needn't handle non-finite values.
Results may differ from the reference program's by a relative error of at most 0.008.
Values may be sent and summed in bfloat16 or wider, within the bound.
A program may use at most 192 MiB of HBM per device.

```python
import jax
import jax.numpy as jnp
import numpy as np
from jax import lax

COMP = 2
S = 4
CYCLES = 2
NX = 32
NY = 128
NZ = 2048


def draw_stencil(key, part):
    shape = (NX, NY, NZ)
    neighbour_diag = jax.random.uniform(jax.random.fold_in(key, 1), (6, 2) + shape, jnp.float32, 0.5, 1.4)
    neighbour_cross = jax.random.uniform(jax.random.fold_in(key, 2), (6, 2) + shape, jnp.float32, -0.3, 0.3)
    centre_cross = jax.random.uniform(jax.random.fold_in(key, 3), (2,) + shape, jnp.float32, -0.5, 0.5)
    margin_value = jax.random.uniform(jax.random.fold_in(key, 4), (2,) + shape, jnp.float32, 0.8, 2.0)
    centre_diag = jnp.sum(neighbour_diag, axis=0) + jnp.sum(jnp.abs(neighbour_cross), axis=0) + jnp.abs(centre_cross) + margin_value
    centre = jnp.stack([centre_diag[0], centre_cross[0], centre_cross[1], centre_diag[1]])
    beside_all = jnp.stack([-neighbour_diag[:, 0], neighbour_cross[:, 0], neighbour_cross[:, 1], -neighbour_diag[:, 1]], axis=1)
    return jnp.concatenate([centre[None], beside_all], axis=0).astype(jnp.bfloat16)


def draw_right_side(key, part):
    shape = (COMP, NX, NY, NZ)
    scales = 10.0 ** jax.random.uniform(jax.random.fold_in(key, 5), shape, jnp.float32, 0.0, 1.0)
    rough = jax.random.truncated_normal(jax.random.fold_in(key, 6), -2.5, 2.5, shape, jnp.float32)
    return rough * scales


def setup_inputs(seed: int = 0) -> dict:
    arg_keys = jax.random.split(jax.random.key(seed), 3)
    stencil = draw_stencil(jax.random.fold_in(arg_keys[2], 71), 0)
    right_side = draw_right_side(jax.random.fold_in(arg_keys[2], 71), 0)
    return dict(stencil=stencil, right_side=right_side)


newton_shifts = (15.0, 2.0, 8.5, 4.75)
basis_scale = 6.5
stencil_offsets = ((1, 1, 1), (0, 1, 1), (2, 1, 1), (1, 0, 1), (1, 2, 1), (1, 1, 0), (1, 1, 2))

def apply_stencil(padded, entries):
    width_x, width_y, width_z = (entries.shape[2], entries.shape[3], entries.shape[4])
    k_result = jnp.zeros((width_x, width_y, width_z), jnp.float32)
    e_result = jnp.zeros((width_x, width_y, width_z), jnp.float32)
    for p, (i, j, k) in enumerate(stencil_offsets):
        shifted = padded[:, i:i + width_x, j:j + width_y, k:k + width_z]
        matrix_block = entries[p].astype(jnp.float32)
        k_result = k_result + matrix_block[0] * shifted[0] + matrix_block[1] * shifted[1]
        e_result = e_result + matrix_block[2] * shifted[0] + matrix_block[3] * shifted[1]
    return jnp.stack([k_result, e_result])

def newton_step(padded, entries, shift_value):
    centre = padded[:, 1:-1, 1:-1, 1:-1]
    return (apply_stencil(padded, entries) - shift_value * centre) / basis_scale

def change_table():
    count = len(newton_shifts)
    table = np.zeros((count + 1, count))
    for j in range(count):
        table[j, j] = newton_shifts[j]
        table[j + 1, j] = basis_scale
    return table

def least_squares(gram_matrix):
    count = len(newton_shifts)
    basis_change = jnp.asarray(change_table(), jnp.float32)
    normal_matrix = jnp.dot(basis_change.T, jnp.dot(gram_matrix, basis_change, precision=lax.Precision.HIGHEST), precision=lax.Precision.HIGHEST)
    normal_rhs = jnp.dot(basis_change.T, gram_matrix[:, 0], precision=lax.Precision.HIGHEST)
    factor = jnp.linalg.cholesky(normal_matrix)
    forward = []
    for i in range(count):
        total = normal_rhs[i]
        for k in range(i):
            total = total - factor[i, k] * forward[k]
        forward.append(total / factor[i, i])
    weights = [forward[0]] * count
    for i in reversed(range(count)):
        total = forward[i]
        for k in range(i + 1, count):
            total = total - factor[k, i] * weights[k]
        weights[i] = total / factor[i, i]
    residual_weights = []
    for j in range(count + 1):
        value = jnp.asarray(1.0 if j == 0 else 0.0, jnp.float32)
        if j < count:
            value = value - newton_shifts[j] * weights[j]
        if j > 0:
            value = value - basis_scale * weights[j - 1]
        residual_weights.append(value)
    return (weights, residual_weights)

def reference(stencil, right_side):
    solution = jnp.zeros_like(right_side)
    residual = right_side
    for cycle in range(CYCLES):
        basis = [residual]
        for j in range(S):
            padded = jnp.pad(basis[j], ((0, 0), (1, 1), (1, 1), (1, 1)))
            basis.append(newton_step(padded, stencil, newton_shifts[j]))
        flat = jnp.stack(basis).reshape(S + 1, -1)
        gram_matrix = jnp.dot(flat, flat.T, precision=lax.Precision.HIGHEST)
        weights, residual_weights = least_squares(gram_matrix)
        for j in range(S):
            solution = solution + weights[j] * basis[j]
        residual = residual_weights[0] * basis[0]
        for j in range(1, S + 1):
            residual = residual + residual_weights[j] * basis[j]
    return (solution, residual)
```

```python
import functools

import jax
import jax.numpy as jnp
from jax import lax
from jax.experimental import pallas as pl
from jax.experimental.pallas import tpu as pltpu
from jax.sharding import PartitionSpec as P

MESH = pl.DeviceIdType.MESH
S = 4
AHEAD = 2
shifts = (15.0, 2.0, 8.5, 4.75)
scale = 6.5
inv = 1.0 / scale

NW = S + 1 + AHEAD
NV = NW + S + 1
PITCH = 40
LANES = 128


def row(x, lt):
    return (2 * x + lt) * PITCH + 8


def kernel(
    sizes, st_hbm, rs_hbm, sol_ref, res_ref,
    st, W, xC, yC, zC, yh, ys, zh, zs, gacc, ar1, ar2, gB, cf,
    load_sem, ssem, rsem, s1sem, r1sem, s2sem, r2sem,
):
    ngx, ngy, ngz = sizes
    gx, gy, gz = (lax.axis_index(a) for a in ("gx", "gy", "gz"))
    NX, NY = 8, 32
    have = (gx > 0, gx < ngx - 1, gy > 0, gy < ngy - 1, gz > 0, gz < ngz - 1)
    beside = (
        {"gx": lax.rem(gx + ngx - 1, ngx)}, {"gx": lax.rem(gx + 1, ngx)},
        {"gy": lax.rem(gy + ngy - 1, ngy)}, {"gy": lax.rem(gy + 1, ngy)},
        {"gz": lax.rem(gz + ngz - 1, ngz)}, {"gz": lax.rem(gz + 1, ngz)},
    )
    line = [{"gz": lax.rem(gz + k, ngz)} for k in range(1, ngz)]
    plane = [
        {"gx": lax.rem(gx + k // ngy, ngx), "gy": lax.rem(gy + k % ngy, ngy)}
        for k in range(1, ngx * ngy)
    ]
    lane = lax.broadcasted_iota(jnp.int32, (NY, LANES), 1)
    zero = jnp.zeros((NY, LANES), jnp.float32)

    loads = [pltpu.make_async_copy(st_hbm, st, load_sem.at[0])]
    for lt in range(2):
        for x in range(NX):
            loads.append(
                pltpu.make_async_copy(
                    rs_hbm.at[:, x, :, pl.ds(lt * LANES, LANES)],
                    W.at[0, :, pl.ds(row(x + 1, lt), NY), :],
                    load_sem.at[1 + lt * NX + x],
                )
            )
    for copy in loads[1:]:
        copy.start()
    loads[0].start()

    barrier = pltpu.get_barrier_semaphore()
    for peer in line + plane:
        pl.semaphore_signal(barrier, inc=1, device_id=peer, device_id_type=MESH)

    for v in range(NV):
        for c in range(2):
            for x in range(1, NX + 1):
                for lt in range(2):
                    W[v, c, pl.ds(row(x, lt) - 8, 8), :] = jnp.zeros((8, LANES), jnp.float32)
            W[v, c, pl.ds(row(NX + 1, 0) - 8, 8), :] = jnp.zeros((8, LANES), jnp.float32)
    for d in range(2):
        @pl.when(jnp.logical_not(have[d]))
        def _():
            for v in range(NV):
                for c in range(2):
                    for lt in range(2):
                        W[v, c, pl.ds(row(0 if d == 0 else NX + 1, lt), NY), :] = zero

        @pl.when(jnp.logical_not(have[2 + d]))
        def _():
            for v in range(NV):
                yh[v, d] = jnp.zeros((2, 2, NX, LANES), jnp.float32)

        @pl.when(jnp.logical_not(have[4 + d]))
        def _():
            for v in range(NV):
                zh[v, d] = zero
    for cyc in range(2):
        gacc[cyc, 15] = jnp.zeros((8, LANES), jnp.float32)

    def x_copy(v, side, lt):
        src = W.at[v, :, pl.ds(row(1 if side == 0 else NX, lt), NY), :]
        dst = W.at[v, :, pl.ds(row(NX + 1 if side == 0 else 0, lt), NY), :]
        k = 2 * side + lt
        return pltpu.make_async_remote_copy(
            src, dst, ssem.at[v, k], rsem.at[v, k], device_id=beside[side], device_id_type=MESH
        )

    def y_copy(v, side):
        k = 4 + side
        return pltpu.make_async_remote_copy(
            ys.at[v, side], yh.at[v, 1 - side], ssem.at[v, k], rsem.at[v, k],
            device_id=beside[2 + side], device_id_type=MESH,
        )

    def z_copy(v, side):
        k = 6 + side
        return pltpu.make_async_remote_copy(
            zs.at[v, side], zh.at[v, 1 - side], ssem.at[v, k], rsem.at[v, k],
            device_id=beside[4 + side], device_id_type=MESH,
        )

    def send_x(v, side, lt):
        @pl.when(have[side])
        def _():
            x_copy(v, side, lt).start()

    def pack_send(v):
        for side in range(2):
            for c in range(2):
                for lt in range(2):
                    ys[v, side, c, lt] = W[
                        v, c, pl.ds(row(1, lt) + (0 if side == 0 else NY - 1), NX, stride=2 * PITCH), :
                    ]

            @pl.when(have[2 + side])
            def _():
                y_copy(v, side).start()
        for side in range(2):
            packed = zero
            for c in range(2):
                for x in range(NX):
                    n = c * NX + x
                    tile = W[v, c, pl.ds(row(x + 1, side), NY), :]
                    turn = n if side == 0 else n + 1
                    if turn:
                        tile = pltpu.roll(tile, turn, 1)
                    packed = jnp.where(lane == n, tile, packed)
            zs[v, side] = packed

            @pl.when(have[4 + side])
            def _():
                z_copy(v, side).start()

    def wait_halo(copy, side, axis):
        @pl.when(have[2 * axis + side])
        def _():
            copy.wait_recv()

    def interior_plane(v, x, left, right, shift):
        out = v + 1
        acc = [[None, None], [None, None]]

        def add(lt, p, b, src):
            for a in range(2):
                term = st[p, 2 * a + b, x - 1, :, lt * LANES:(lt + 1) * LANES].astype(jnp.float32) * src
                acc[lt][a] = term if acc[lt][a] is None else acc[lt][a] + term

        def at(b, xx, lt, off=0):
            start = row(xx, lt)
            if off == 0 and not isinstance(start, int):
                start = pl.multiple_of(start, 8)
            return W[v, b, pl.ds(start + off, NY), :]

        for b in range(2):
            centre = [at(b, x, lt) for lt in range(2)]
            up = [pltpu.roll(t, 1, 1) for t in centre]
            down = [pltpu.roll(t, LANES - 1, 1) for t in centre]
            for lt in range(2):
                add(lt, 0, b, centre[lt])
            add(0, 5, b, jnp.where(lane == 0, 0.0, up[0]))
            add(1, 5, b, jnp.where(lane == 0, up[0], up[1]))
            add(0, 6, b, jnp.where(lane == LANES - 1, down[1], down[0]))
            add(1, 6, b, jnp.where(lane == LANES - 1, 0.0, down[1]))
            for lt in range(2):
                if left:
                    add(lt, 1, b, at(b, x - 1, lt))
                if right:
                    add(lt, 2, b, at(b, x + 1, lt))
                add(lt, 3, b, at(b, x, lt, -1))
                add(lt, 4, b, at(b, x, lt, 1))
        for lt in range(2):
            for a in range(2):
                start = row(x, lt)
                if not isinstance(start, int):
                    start = pl.multiple_of(start, 8)
                W[out, a, pl.ds(start, NY), :] = (acc[lt][a] - shift * at(a, x, lt)) * inv

    def interior(v, shift):
        interior_plane(v, 1, False, True, shift)

        def body(x, carry):
            interior_plane(v, x, True, True, shift)
            return carry

        lax.fori_loop(2, NX, body, 0)
        interior_plane(v, NX, True, False, shift)

    def fix_y(v):
        out = v + 1
        for side in range(2):
            for lt in range(2):
                h = [yh[v, side, b, lt] for b in range(2)]
                for a in range(2):
                    part = yC[side, 2 * a, lt] * h[0] + yC[side, 2 * a + 1, lt] * h[1]
                    rows = pl.ds(row(1, lt) + (0 if side == 0 else NY - 1), NX, stride=2 * PITCH)
                    W[out, a, rows, :] = W[out, a, rows, :] + part

    def fix_z(v):
        out = v + 1
        for side in range(2):
            h = zh[v, side]
            other = jnp.where(lane < NX, pltpu.roll(h, LANES - NX, 1), pltpu.roll(h, NX, 1))
            part = zC[side, 0] * h + zC[side, 1] * other
            edge = 0 if side == 0 else LANES - 1
            for a in range(2):
                for x in range(NX):
                    turn = (edge - (a * NX + x)) % LANES
                    moved = pltpu.roll(part, turn, 1) if turn else part
                    rows = pl.ds(row(x + 1, side), NY)
                    W[out, a, rows, :] = W[out, a, rows, :] + jnp.where(lane == edge, moved, 0.0)

    def fix_x(v, side, lt):
        out = v + 1
        src = row(0 if side == 0 else NX + 1, lt)
        dst = pl.ds(row(1 if side == 0 else NX, lt), NY)
        h = [W[v, b, pl.ds(src, NY), :] for b in range(2)]
        for a in range(2):
            part = xC[side, 2 * a, lt] * h[0] + xC[side, 2 * a + 1, lt] * h[1]
            W[out, a, dst, :] = W[out, a, dst, :] + part

    def finish(v, sent, local):
        if not local:
            for side in range(2):
                wait_halo(y_copy(v, 1 - side), side, 1)
                wait_halo(z_copy(v, 1 - side), side, 2)
        fix_y(v)
        fix_z(v)
        for lt in range(2):
            for side in range(2):
                if not local:
                    wait_halo(x_copy(v, 1 - side, lt), side, 0)
                fix_x(v, side, lt)
                if sent:
                    send_x(v + 1, side, lt)
        if sent:
            pack_send(v + 1)

    def gram_row(cyc, first, j):
        def body(x, accs):
            accs = list(accs)
            for c in range(2):
                for lt in range(2):
                    rows = pl.ds(pl.multiple_of(row(x, lt), 8), NY)
                    right = W[first + j, c, rows, :]
                    for i in range(j + 1):
                        left = right if i == j else W[first + i, c, rows, :]
                        accs[i] = accs[i] + jnp.sum((left * right).reshape(NY // 8, 8, LANES), axis=0)
            return tuple(accs)

        accs = lax.fori_loop(1, NX + 1, body, tuple(jnp.zeros((8, LANES), jnp.float32) for _ in range(j + 1)))
        for i in range(j + 1):
            gacc[cyc, j * (j + 1) // 2 + i] = accs[i]

    def line_copy(cyc, k):
        return pltpu.make_async_remote_copy(
            ar1.at[cyc, gz], ar1.at[cyc, gz], s1sem.at[cyc, k], r1sem.at[cyc, k],
            device_id=line[k], device_id_type=MESH,
        )

    def plane_copy(cyc, k):
        slot = gx * ngy + gy
        return pltpu.make_async_remote_copy(
            ar2.at[cyc, slot], ar2.at[cyc, slot], s2sem.at[cyc, k], r2sem.at[cyc, k],
            device_id=plane[k], device_id_type=MESH,
        )

    def reduce_start(cyc):
        ar1[cyc, gz] = jnp.sum(gacc[cyc], axis=1)
        for k in range(ngz - 1):
            line_copy(cyc, k).start()

    def reduce_middle(cyc):
        for k in range(ngz - 1):
            line_copy(cyc, k).wait_recv()
        ar2[cyc, gx * ngy + gy] = jnp.sum(ar1[cyc], axis=0)
        for k in range(ngx * ngy - 1):
            plane_copy(cyc, k).start()

    def reduce_end(cyc):
        for k in range(ngx * ngy - 1):
            plane_copy(cyc, k).wait_recv()
        total = jnp.sum(ar2[cyc], axis=0)
        gB[cyc] = jnp.broadcast_to(jnp.sum(total, axis=1, keepdims=True), (16, LANES))

    def solve(cyc):
        def G(i, j):
            i, j = min(i, j), max(i, j)
            return jnp.broadcast_to(gB[cyc, pl.ds(j * (j + 1) // 2 + i, 1), :], (8, LANES))

        g = [[G(i, j) for j in range(S + 1)] for i in range(S + 1)]
        gb = [[shifts[j] * g[i][j] + scale * g[i][j + 1] for j in range(S)] for i in range(S + 1)]
        h = [[shifts[i] * gb[i][j] + scale * gb[i + 1][j] if j <= i else None for j in range(S)] for i in range(S)]
        rhs = [gb[0][i] for i in range(S)]
        low = [[None] * S for _ in range(S)]
        dinv = [None] * S
        full = [[None] * S for _ in range(S)]
        for j in range(S):
            d = h[j][j]
            for k in range(j):
                d = d - low[j][k] * full[j][k]
            dinv[j] = 1.0 / d
            for i in range(j + 1, S):
                t = h[i][j]
                for k in range(j):
                    t = t - full[i][k] * low[j][k]
                full[i][j] = t
                low[i][j] = t * dinv[j]
        fwd = []
        for i in range(S):
            t = rhs[i]
            for k in range(i):
                t = t - low[i][k] * fwd[k]
            fwd.append(t)
        y = [None] * S
        for i in reversed(range(S)):
            t = fwd[i] * dinv[i]
            for k in range(i + 1, S):
                t = t - low[k][i] * y[k]
            y[i] = t
        c = []
        for j in range(S + 1):
            t = jnp.full((8, LANES), 1.0 if j == 0 else 0.0, jnp.float32)
            if j < S:
                t = t - shifts[j] * y[j]
            if j > 0:
                t = t - scale * y[j - 1]
            c.append(t)
        return y, c

    def put(n, value):
        cf[pl.ds(n, 1), :] = value[0:1]

    def coef(n):
        return cf[pl.ds(n, 1), :]

    for copy in loads[1:]:
        copy.wait()
    pl.semaphore_wait(barrier, ngz - 1 + ngx * ngy - 1)
    for lt in range(2):
        for side in range(2):
            send_x(0, side, lt)
    pack_send(0)
    loads[0].wait()

    for side in range(2):
        for e in range(4):
            for lt in range(2):
                lanes = slice(lt * LANES, (lt + 1) * LANES)
                xC[side, e, lt] = st[1 + side, e, 0 if side == 0 else NX - 1, :, lanes].astype(jnp.float32) * inv
                for x in range(NX):
                    part = st[3 + side, e, x, 16 * side:16 * side + 16, lanes].astype(jnp.float32) * inv
                    yC[side, e, lt, pl.ds(x, 1), :] = part[0:1] if side == 0 else part[15:16]
        lanes = slice(side * LANES, (side + 1) * LANES)
        for kind in range(2):
            packed = zero
            for c in range(2):
                e = 3 * c if kind == 0 else c + 1
                for x in range(NX):
                    n = c * NX + x
                    tile = st[5 + side, e, x, :, lanes].astype(jnp.float32) * inv
                    turn = n if side == 0 else n + 1
                    if turn:
                        tile = pltpu.roll(tile, turn, 1)
                    packed = jnp.where(lane == n, tile, packed)
            zC[side, kind] = packed

    for j in range(S + AHEAD):
        interior(j, shifts[j % S])
        if j < S:
            gram_row(0, 0, j)
        finish(j, True, False)
        if j + 1 == S:
            gram_row(0, 0, S)
            reduce_start(0)
        if j + 1 == S + 1:
            reduce_middle(0)
    if AHEAD == 0:
        reduce_middle(0)
    reduce_end(0)
    y, c = solve(0)
    for k in range(S):
        put(k, y[k])
    combo = [c + [None] * AHEAD]
    for j in range(AHEAD):
        old, new = combo[-1], []
        for k in range(NW):
            t = old[k - 1] if k > 0 else None
            factor = (shifts[k % S] - shifts[j]) * inv
            if old[k] is not None and factor != 0.0:
                t = factor * old[k] if t is None else t + factor * old[k]
            new.append(t)
        combo.append(new)
    place = {}
    for j in range(AHEAD + 1):
        for k in range(NW):
            if combo[j][k] is not None:
                place[j, k] = 8 + j * 8 + k
                put(place[j, k], combo[j][k])

    def combine(j, get):
        t = None
        for k in range(NW):
            if (j, k) in place:
                term = coef(place[j, k]) * get(k)
                t = term if t is None else t + term
        return t

    def second(x, carry):
        for cc in range(2):
            for lt in range(2):
                rows = pl.ds(pl.multiple_of(row(x, lt), 8), NY)
                tiles = [W[k, cc, rows, :] for k in range(NW)]
                for j in range(AHEAD + 1):
                    W[NW + j, cc, rows, :] = combine(j, lambda k: tiles[k])
        return carry

    lax.fori_loop(1, NX + 1, second, 0)
    last = NW + AHEAD
    interior(last, shifts[AHEAD])
    for side in range(2):
        wait_halo(y_copy(NW - 1, 1 - side), side, 1)
        wait_halo(z_copy(NW - 1, 1 - side), side, 2)
        for lt in range(2):
            wait_halo(x_copy(NW - 1, 1 - side, lt), side, 0)
    for side in range(2):
        for cc in range(2):
            for lt in range(2):
                rows = pl.ds(row(0 if side == 0 else NX + 1, lt), NY)
                W[last, cc, rows, :] = combine(AHEAD, lambda k: W[k, cc, rows, :])
                yh[last, side, cc, lt] = combine(AHEAD, lambda k: yh[k, side, cc, lt])
        zh[last, side] = combine(AHEAD, lambda k: zh[k, side])
    finish(last, True, True)
    for j in range(AHEAD + 1):
        gram_row(1, NW, j)

    for j in range(AHEAD + 1, S):
        v = NW + j
        interior(v, shifts[j])
        gram_row(1, NW, j)
        finish(v, j + 1 < S, False)
    gram_row(1, NW, S)
    reduce_start(1)

    def first_share(x, carry):
        for cc in range(2):
            for lt in range(2):
                rows = pl.ds(pl.multiple_of(row(x, lt), 8), NY)
                t = coef(0) * W[0, cc, rows, :]
                for k in range(1, S):
                    t = t + coef(k) * W[k, cc, rows, :]
                sol_ref[cc, x - 1, :, lt * LANES:(lt + 1) * LANES] = t
        return carry

    lax.fori_loop(1, NX + 1, first_share, 0)
    reduce_middle(1)
    reduce_end(1)
    y, c = solve(1)
    for k in range(S):
        put(k, y[k])
    for k in range(S + 1):
        put(8 + k, c[k])

    def final(x, carry):
        for cc in range(2):
            for lt in range(2):
                rows = pl.ds(pl.multiple_of(row(x, lt), 8), NY)
                lanes = slice(lt * LANES, (lt + 1) * LANES)
                tile = W[NW, cc, rows, :]
                s = sol_ref[cc, x - 1, :, lanes] + coef(0) * tile
                r = coef(8) * tile
                for k in range(1, S + 1):
                    tile = W[NW + k, cc, rows, :]
                    if k < S:
                        s = s + coef(k) * tile
                    r = r + coef(8 + k) * tile
                sol_ref[cc, x - 1, :, lanes] = s
                res_ref[cc, x - 1, :, lanes] = r
        return carry

    lax.fori_loop(1, NX + 1, final, 0)

    for v in list(range(NW)) + list(range(last + 1, NW + S)):
        for side in range(2):
            @pl.when(have[side])
            def _():
                for lt in range(2):
                    x_copy(v, side, lt).wait_send()

            @pl.when(have[2 + side])
            def _():
                y_copy(v, side).wait_send()

            @pl.when(have[4 + side])
            def _():
                z_copy(v, side).wait_send()
    for cyc in range(2):
        for k in range(ngz - 1):
            line_copy(cyc, k).wait_send()
        for k in range(ngx * ngy - 1):
            plane_copy(cyc, k).wait_send()


def solution(mesh):
    sizes = tuple(mesh.shape[a] for a in ("gx", "gy", "gz"))
    ngx, ngy, ngz = sizes

    def on_device(stencil, right_side):
        f32 = jnp.float32
        out = jax.ShapeDtypeStruct(right_side.shape, f32)
        dma = pltpu.SemaphoreType.DMA
        return pl.pallas_call(
            functools.partial(kernel, sizes),
            out_shape=(out, out),
            in_specs=[pl.BlockSpec(memory_space=pl.ANY)] * 2,
            out_specs=(pl.BlockSpec(memory_space=pltpu.VMEM),) * 2,
            scratch_shapes=[
                pltpu.VMEM(stencil.shape, stencil.dtype),
                pltpu.VMEM((NV, 2, 20 * PITCH + 8, LANES), f32),
                pltpu.VMEM((2, 4, 2, 32, LANES), f32),
                pltpu.VMEM((2, 4, 2, 8, LANES), f32),
                pltpu.VMEM((2, 2, 32, LANES), f32),
                pltpu.VMEM((NV, 2, 2, 2, 8, LANES), f32),
                pltpu.VMEM((NV, 2, 2, 2, 8, LANES), f32),
                pltpu.VMEM((NV, 2, 32, LANES), f32),
                pltpu.VMEM((NV, 2, 32, LANES), f32),
                pltpu.VMEM((2, 16, 8, LANES), f32),
                pltpu.VMEM((2, ngz, 16, LANES), f32),
                pltpu.VMEM((2, ngx * ngy, 16, LANES), f32),
                pltpu.VMEM((2, 16, LANES), f32),
                pltpu.VMEM((40, LANES), f32),
                dma((17,)),
                dma((NV, 8)),
                dma((NV, 8)),
                dma((2, ngz - 1)),
                dma((2, ngz - 1)),
                dma((2, ngx * ngy - 1)),
                dma((2, ngx * ngy - 1)),
            ],
            compiler_params=pltpu.CompilerParams(
                collective_id=0, has_side_effects=True, vmem_limit_bytes=48 << 20
            ),
            name="gmres",
        )(stencil, right_side)

    specs = (P(None, None, "gx", "gy", "gz"), P(None, "gx", "gy", "gz"))
    return jax.shard_map(
        on_device, mesh=mesh, in_specs=specs, out_specs=(specs[1], specs[1]), check_vma=False
    )
```

```python
import functools

import jax
import jax.numpy as jnp
from jax import lax
from jax.experimental import pallas as pl
from jax.experimental.pallas import tpu as pltpu
from jax.sharding import PartitionSpec as P

MESH = pl.DeviceIdType.MESH
S = 4
AHEAD = 2
shifts = (15.0, 2.0, 8.5, 4.75)
scale = 6.5
inv = 1.0 / scale

NW = S + 1 + AHEAD
NV = NW + S + 1
PITCH = 40
LANES = 128


def row(x, lt):
    return (2 * x + lt) * PITCH + 8


def kernel(
    sizes, st_hbm, rs_hbm, sol_ref, res_ref,
    st, W, xC, yC, eC, yh, ys, eh, eb, gacc, ar1, ar2, gB, cf,
    load_sem, ssem, rsem, s1sem, r1sem, s2sem, r2sem,
):
    ngx, ngy, ngz = sizes
    gx, gy, gz = (lax.axis_index(a) for a in ("gx", "gy", "gz"))
    NX, NY = 8, 32
    have = (gx > 0, gx < ngx - 1, gy > 0, gy < ngy - 1, gz > 0, gz < ngz - 1)
    beside = (
        {"gx": lax.rem(gx + ngx - 1, ngx)}, {"gx": lax.rem(gx + 1, ngx)},
        {"gy": lax.rem(gy + ngy - 1, ngy)}, {"gy": lax.rem(gy + 1, ngy)},
        {"gz": lax.rem(gz + ngz - 1, ngz)}, {"gz": lax.rem(gz + 1, ngz)},
    )
    line = [{"gz": lax.rem(gz + k, ngz)} for k in range(1, ngz)]
    plane = [
        {"gx": lax.rem(gx + k // ngy, ngx), "gy": lax.rem(gy + k % ngy, ngy)}
        for k in range(1, ngx * ngy)
    ]
    lane = lax.broadcasted_iota(jnp.int32, (NY, LANES), 1)
    lane8 = lax.broadcasted_iota(jnp.int32, (8, LANES), 1)
    sub8 = lax.broadcasted_iota(jnp.int32, (8, LANES), 0)
    eye = lax.broadcasted_iota(jnp.int32, (16, LANES), 1) == lax.broadcasted_iota(jnp.int32, (16, LANES), 0)
    zero = jnp.zeros((NY, LANES), jnp.float32)

    loads = [pltpu.make_async_copy(st_hbm, st, load_sem.at[0])]
    for lt in range(2):
        for x in range(NX):
            loads.append(
                pltpu.make_async_copy(
                    rs_hbm.at[:, x, :, pl.ds(lt * LANES, LANES)],
                    W.at[0, :, pl.ds(row(x + 1, lt), NY), :],
                    load_sem.at[1 + lt * NX + x],
                )
            )
    for copy in loads[1:]:
        copy.start()
    loads[0].start()

    barrier = pltpu.get_barrier_semaphore()
    for peer in line + plane:
        pl.semaphore_signal(barrier, inc=1, device_id=peer, device_id_type=MESH)

    for v in range(NV):
        for c in range(2):
            for x in range(1, NX + 1):
                for lt in range(2):
                    W[v, c, pl.ds(row(x, lt) - 8, 8), :] = jnp.zeros((8, LANES), jnp.float32)
            W[v, c, pl.ds(row(NX + 1, 0) - 8, 8), :] = jnp.zeros((8, LANES), jnp.float32)
    for d in range(2):
        @pl.when(jnp.logical_not(have[d]))
        def _():
            for v in range(NV):
                for c in range(2):
                    for lt in range(2):
                        W[v, c, pl.ds(row(0 if d == 0 else NX + 1, lt), NY), :] = zero

        @pl.when(jnp.logical_not(have[2 + d]))
        def _():
            for v in range(NV):
                yh[v, d] = jnp.zeros((2, 2, NX, LANES), jnp.float32)

    for d in range(6):
        @pl.when(jnp.logical_not(have[d]))
        def _():
            for v in range(NV):
                eh[v, d] = jnp.zeros((8, LANES), jnp.float32)

    for cyc in range(2):
        gacc[cyc, 15] = jnp.zeros((8, LANES), jnp.float32)

    def x_copy(v, side, lt):
        src = W.at[v, :, pl.ds(row(1 if side == 0 else NX, lt), NY), :]
        dst = W.at[v, :, pl.ds(row(NX + 1 if side == 0 else 0, lt), NY), :]
        k = 2 * side + lt
        return pltpu.make_async_remote_copy(
            src, dst, ssem.at[v, k], rsem.at[v, k], device_id=beside[side], device_id_type=MESH
        )

    def y_copy(v, side):
        k = 4 + side
        return pltpu.make_async_remote_copy(
            ys.at[v, side], yh.at[v, 1 - side], ssem.at[v, k], rsem.at[v, k],
            device_id=beside[2 + side], device_id_type=MESH,
        )

    def e_copy(v, d):
        return pltpu.make_async_remote_copy(
            eb.at[v], eh.at[v, d ^ 1], ssem.at[v, 6 + d], rsem.at[v, 6 + d],
            device_id=beside[d], device_id_type=MESH,
        )

    def send_x(v, side, lt):
        @pl.when(have[side])
        def _():
            x_copy(v, side, lt).start()

    def send_y(v):
        for side in range(2):
            for c in range(2):
                for lt in range(2):
                    ys[v, side, c, lt] = W[
                        v, c, pl.ds(row(1, lt) + (0 if side == 0 else NY - 1), NX, stride=2 * PITCH), :
                    ]

            @pl.when(have[2 + side])
            def _():
                y_copy(v, side).start()

    def send_edges(v):
        for d in range(6):
            @pl.when(have[d])
            def _():
                e_copy(v, d).start()

    def place_edge(packed, tile, side, t, c, x):
        n = side * 64 + t * 16 + c * 8 + x
        turn = n if side == 0 else (n + 1) % LANES
        tile = tile[8 * t:8 * t + 8]
        if turn:
            tile = pltpu.roll(tile, turn, 1)
        return jnp.where(lane8 == n, tile, packed)

    def pack_edges(v):
        packed = jnp.zeros((8, LANES), jnp.float32)
        for side in range(2):
            for c in range(2):
                for x in range(NX):
                    tile = W[v, c, pl.ds(row(x + 1, side), NY), :]
                    for t in range(4):
                        packed = place_edge(packed, tile, side, t, c, x)
        eb[v] = packed

    def unpack_edges(v, planes):
        packed = eb[v]
        for side in range(2):
            edge = 0 if side == 0 else LANES - 1
            for c in range(2):
                for x in planes:
                    for t in range(4):
                        turn = (edge - (side * 64 + t * 16 + c * 8 + x)) % LANES
                        moved = pltpu.roll(packed, turn, 1) if turn else packed
                        rows = pl.ds(row(x + 1, side) + 8 * t, 8)
                        W[v, c, rows, :] = jnp.where(lane8 == edge, moved, W[v, c, rows, :])

    def swapped(h):
        return jnp.where((lane8 & 8) == 0, pltpu.roll(h, LANES - 8, 1), pltpu.roll(h, 8, 1))

    def fix_edges(v):
        hz = pltpu.roll(jnp.where(lane8 < 64, eh[v, 5], eh[v, 4]), 64, 1)
        hy = jnp.where(
            sub8 == 0,
            pltpu.roll(pltpu.roll(eh[v, 2], LANES - 48, 1), 1, 0),
            pltpu.roll(pltpu.roll(eh[v, 3], 48, 1), 7, 0),
        )
        hx = jnp.where((lane8 & 7) == 0, pltpu.roll(eh[v, 0], LANES - 7, 1), pltpu.roll(eh[v, 1], 7, 1))
        part = eb[v + 1]
        for axis, h in enumerate((hx, hy, hz)):
            part = part + (eC[axis, 0] * h + eC[axis, 1] * swapped(h))
        eb[v + 1] = part

    def wait_halo(copy, side, axis):
        @pl.when(have[2 * axis + side])
        def _():
            copy.wait_recv()

    def wait_edges(v, d):
        @pl.when(have[d])
        def _():
            e_copy(v, d ^ 1).wait_recv()

    def interior_plane(v, x, left, right, shift):
        out = v + 1
        acc = [[None, None], [None, None]]

        def add(lt, p, b, src):
            for a in range(2):
                term = st[p, 2 * a + b, x - 1, :, lt * LANES:(lt + 1) * LANES].astype(jnp.float32) * src
                acc[lt][a] = term if acc[lt][a] is None else acc[lt][a] + term

        def at(b, xx, lt, off=0):
            start = row(xx, lt)
            if off == 0 and not isinstance(start, int):
                start = pl.multiple_of(start, 8)
            return W[v, b, pl.ds(start + off, NY), :]

        for b in range(2):
            centre = [at(b, x, lt) for lt in range(2)]
            up = [pltpu.roll(t, 1, 1) for t in centre]
            down = [pltpu.roll(t, LANES - 1, 1) for t in centre]
            for lt in range(2):
                add(lt, 0, b, centre[lt])
            add(0, 5, b, jnp.where(lane == 0, 0.0, up[0]))
            add(1, 5, b, jnp.where(lane == 0, up[0], up[1]))
            add(0, 6, b, jnp.where(lane == LANES - 1, down[1], down[0]))
            add(1, 6, b, jnp.where(lane == LANES - 1, 0.0, down[1]))
            for lt in range(2):
                if left:
                    add(lt, 1, b, at(b, x - 1, lt))
                if right:
                    add(lt, 2, b, at(b, x + 1, lt))
                add(lt, 3, b, at(b, x, lt, -1))
                add(lt, 4, b, at(b, x, lt, 1))
        for lt in range(2):
            for a in range(2):
                start = row(x, lt)
                if not isinstance(start, int):
                    start = pl.multiple_of(start, 8)
                W[out, a, pl.ds(start, NY), :] = (acc[lt][a] - shift * at(a, x, lt)) * inv

    def interior(v, shift):
        interior_plane(v, 1, False, True, shift)

        def body(x, carry):
            interior_plane(v, x, True, True, shift)
            return carry

        lax.fori_loop(2, NX, body, 0)
        interior_plane(v, NX, True, False, shift)
        pack_edges(v + 1)

    def fix_y(v):
        out = v + 1
        for side in range(2):
            for lt in range(2):
                h = [yh[v, side, b, lt] for b in range(2)]
                for a in range(2):
                    part = yC[side, 2 * a, lt] * h[0] + yC[side, 2 * a + 1, lt] * h[1]
                    rows = pl.ds(row(1, lt) + (0 if side == 0 else NY - 1), NX, stride=2 * PITCH)
                    W[out, a, rows, :] = W[out, a, rows, :] + part

    def fix_x(v, side, lt):
        out = v + 1
        src = row(0 if side == 0 else NX + 1, lt)
        dst = pl.ds(row(1 if side == 0 else NX, lt), NY)
        h = [W[v, b, pl.ds(src, NY), :] for b in range(2)]
        for a in range(2):
            part = xC[side, 2 * a, lt] * h[0] + xC[side, 2 * a + 1, lt] * h[1]
            W[out, a, dst, :] = W[out, a, dst, :] + part

    def finish(v, sent, local):
        if not local:
            for d in range(6):
                wait_edges(v, d)
        fix_edges(v)
        if sent:
            send_edges(v + 1)
        unpack_edges(v + 1, (0, NX - 1))
        if not local:
            for side in range(2):
                wait_halo(y_copy(v, 1 - side), side, 1)
        fix_y(v)
        for lt in range(2):
            for side in range(2):
                if not local:
                    wait_halo(x_copy(v, 1 - side, lt), side, 0)
                fix_x(v, side, lt)
                if sent:
                    send_x(v + 1, side, lt)
        if sent:
            send_y(v + 1)
        unpack_edges(v + 1, range(1, NX - 1))

    def gram_row(cyc, first, j):
        def body(x, accs):
            accs = list(accs)
            for c in range(2):
                for lt in range(2):
                    rows = pl.ds(pl.multiple_of(row(x, lt), 8), NY)
                    right = W[first + j, c, rows, :]
                    for i in range(j + 1):
                        left = right if i == j else W[first + i, c, rows, :]
                        accs[i] = accs[i] + jnp.sum((left * right).reshape(NY // 8, 8, LANES), axis=0)
            return tuple(accs)

        accs = lax.fori_loop(1, NX + 1, body, tuple(jnp.zeros((8, LANES), jnp.float32) for _ in range(j + 1)))
        for i in range(j + 1):
            gacc[cyc, j * (j + 1) // 2 + i] = accs[i]

    def line_copy(cyc, k):
        return pltpu.make_async_remote_copy(
            ar1.at[cyc, gz], ar1.at[cyc, gz], s1sem.at[cyc, k], r1sem.at[cyc, k],
            device_id=line[k], device_id_type=MESH,
        )

    def plane_copy(cyc, k):
        slot = gx * ngy + gy
        return pltpu.make_async_remote_copy(
            ar2.at[cyc, slot], ar2.at[cyc, slot], s2sem.at[cyc, k], r2sem.at[cyc, k],
            device_id=plane[k], device_id_type=MESH,
        )

    def reduce_start(cyc):
        rows = jnp.sum(jnp.sum(gacc[cyc], axis=1), axis=1, keepdims=True)
        ar1[cyc, gz] = jnp.sum(jnp.where(eye, rows, 0.0), axis=0, keepdims=True)
        for k in range(ngz - 1):
            line_copy(cyc, k).start()

    def reduce_middle(cyc):
        for k in range(ngz - 1):
            line_copy(cyc, k).wait_recv()
        ar2[cyc, gx * ngy + gy] = jnp.sum(ar1[cyc], axis=0)
        for k in range(ngx * ngy - 1):
            plane_copy(cyc, k).start()

    def reduce_end(cyc):
        for k in range(ngx * ngy - 1):
            plane_copy(cyc, k).wait_recv()
        total = jnp.sum(ar2[cyc], axis=0)
        rows = jnp.sum(jnp.where(eye, total, 0.0), axis=1, keepdims=True)
        gB[cyc] = jnp.broadcast_to(rows, (16, LANES))

    def solve(cyc):
        def G(i, j):
            i, j = min(i, j), max(i, j)
            return jnp.broadcast_to(gB[cyc, pl.ds(j * (j + 1) // 2 + i, 1), :], (8, LANES))

        g = [[G(i, j) for j in range(S + 1)] for i in range(S + 1)]
        gb = [[shifts[j] * g[i][j] + scale * g[i][j + 1] for j in range(S)] for i in range(S + 1)]
        h = [[shifts[i] * gb[i][j] + scale * gb[i + 1][j] if j <= i else None for j in range(S)] for i in range(S)]
        rhs = [gb[0][i] for i in range(S)]
        low = [[None] * S for _ in range(S)]
        dinv = [None] * S
        full = [[None] * S for _ in range(S)]
        for j in range(S):
            d = h[j][j]
            for k in range(j):
                d = d - low[j][k] * full[j][k]
            dinv[j] = 1.0 / d
            for i in range(j + 1, S):
                t = h[i][j]
                for k in range(j):
                    t = t - full[i][k] * low[j][k]
                full[i][j] = t
                low[i][j] = t * dinv[j]
        fwd = []
        for i in range(S):
            t = rhs[i]
            for k in range(i):
                t = t - low[i][k] * fwd[k]
            fwd.append(t)
        y = [None] * S
        for i in reversed(range(S)):
            t = fwd[i] * dinv[i]
            for k in range(i + 1, S):
                t = t - low[k][i] * y[k]
            y[i] = t
        c = []
        for j in range(S + 1):
            t = jnp.full((8, LANES), 1.0 if j == 0 else 0.0, jnp.float32)
            if j < S:
                t = t - shifts[j] * y[j]
            if j > 0:
                t = t - scale * y[j - 1]
            c.append(t)
        return y, c

    def put(n, value):
        cf[pl.ds(n, 1), :] = value[0:1]

    def coef(n):
        return cf[pl.ds(n, 1), :]

    for copy in loads[1:]:
        copy.wait()
    pack_edges(0)
    pl.semaphore_wait(barrier, ngz - 1 + ngx * ngy - 1)
    for lt in range(2):
        for side in range(2):
            send_x(0, side, lt)
    send_edges(0)
    send_y(0)
    loads[0].wait()

    def entry(p, e, x, lt):
        return st[p, e, x, :, lt * LANES:(lt + 1) * LANES].astype(jnp.float32) * inv

    for side in range(2):
        for e in range(4):
            for lt in range(2):
                edge = 0 if lt == 0 else LANES - 1
                xC[side, e, lt] = jnp.where(lane == edge, 0.0, entry(1 + side, e, 0 if side == 0 else NX - 1, lt))
                for x in range(NX):
                    part = st[3 + side, e, x, 16 * side:16 * side + 16, lt * LANES:(lt + 1) * LANES]
                    part = jnp.where(lane[:16] == edge, 0.0, part.astype(jnp.float32) * inv)
                    yC[side, e, lt, pl.ds(x, 1), :] = part[0:1] if side == 0 else part[15:16]
    for kind in range(2):
        ex, ey, ez = (jnp.zeros((8, LANES), jnp.float32),) * 3
        for side in range(2):
            for c in range(2):
                e = 3 * c if kind == 0 else c + 1
                for x in range(NX):
                    tile = entry(5 + side, e, x, side)
                    for t in range(4):
                        ez = place_edge(ez, tile, side, t, c, x)
                    ey = place_edge(ey, entry(3, e, x, side), side, 0, c, x)
                    ey = place_edge(ey, entry(4, e, x, side), side, 3, c, x)
                for p, x in ((1, 0), (2, NX - 1)):
                    tile = entry(p, e, x, side)
                    for t in range(4):
                        ex = place_edge(ex, tile, side, t, c, x)
        tile_y = (lane8 // 16) % 4
        inside = jnp.logical_or(
            jnp.logical_and(tile_y == 0, sub8 == 0), jnp.logical_and(tile_y == 3, sub8 == 7)
        )
        eC[0, kind] = ex
        eC[1, kind] = jnp.where(inside, ey, 0.0)
        eC[2, kind] = ez

    for j in range(S + AHEAD):
        interior(j, shifts[j % S])
        if j < S:
            gram_row(0, 0, j)
        finish(j, True, False)
        if j + 1 == S:
            gram_row(0, 0, S)
            reduce_start(0)
        if j + 1 == S + 1:
            reduce_middle(0)
    if AHEAD == 0:
        reduce_middle(0)
    reduce_end(0)
    y, c = solve(0)
    for k in range(S):
        put(k, y[k])
    combo = [c + [None] * AHEAD]
    for j in range(AHEAD):
        old, new = combo[-1], []
        for k in range(NW):
            t = old[k - 1] if k > 0 else None
            factor = (shifts[k % S] - shifts[j]) * inv
            if old[k] is not None and factor != 0.0:
                t = factor * old[k] if t is None else t + factor * old[k]
            new.append(t)
        combo.append(new)
    place = {}
    for j in range(AHEAD + 1):
        for k in range(NW):
            if combo[j][k] is not None:
                place[j, k] = 8 + j * 8 + k
                put(place[j, k], combo[j][k])

    def combine(j, get):
        t = None
        for k in range(NW):
            if (j, k) in place:
                term = coef(place[j, k]) * get(k)
                t = term if t is None else t + term
        return t

    def second(x, carry):
        for cc in range(2):
            for lt in range(2):
                rows = pl.ds(pl.multiple_of(row(x, lt), 8), NY)
                tiles = [W[k, cc, rows, :] for k in range(NW)]
                for j in range(AHEAD + 1):
                    W[NW + j, cc, rows, :] = combine(j, lambda k: tiles[k])
        return carry

    lax.fori_loop(1, NX + 1, second, 0)
    last = NW + AHEAD
    interior(last, shifts[AHEAD])
    for side in range(2):
        wait_halo(y_copy(NW - 1, 1 - side), side, 1)
        for lt in range(2):
            wait_halo(x_copy(NW - 1, 1 - side, lt), side, 0)
    for d in range(6):
        wait_edges(NW - 1, d)
        eh[last, d] = combine(AHEAD, lambda k: eh[k, d])
    for side in range(2):
        for cc in range(2):
            for lt in range(2):
                rows = pl.ds(row(0 if side == 0 else NX + 1, lt), NY)
                W[last, cc, rows, :] = combine(AHEAD, lambda k: W[k, cc, rows, :])
                yh[last, side, cc, lt] = combine(AHEAD, lambda k: yh[k, side, cc, lt])
    finish(last, True, True)
    for j in range(AHEAD + 1):
        gram_row(1, NW, j)

    for j in range(AHEAD + 1, S):
        v = NW + j
        interior(v, shifts[j])
        gram_row(1, NW, j)
        finish(v, j + 1 < S, False)
    gram_row(1, NW, S)
    reduce_start(1)

    def first_share(x, carry):
        for cc in range(2):
            for lt in range(2):
                rows = pl.ds(pl.multiple_of(row(x, lt), 8), NY)
                t = coef(0) * W[0, cc, rows, :]
                for k in range(1, S):
                    t = t + coef(k) * W[k, cc, rows, :]
                sol_ref[cc, x - 1, :, lt * LANES:(lt + 1) * LANES] = t
        return carry

    lax.fori_loop(1, NX + 1, first_share, 0)
    reduce_middle(1)
    reduce_end(1)
    y, c = solve(1)
    for k in range(S):
        put(k, y[k])
    for k in range(S + 1):
        put(8 + k, c[k])

    def final(x, carry):
        for cc in range(2):
            for lt in range(2):
                rows = pl.ds(pl.multiple_of(row(x, lt), 8), NY)
                lanes = slice(lt * LANES, (lt + 1) * LANES)
                tile = W[NW, cc, rows, :]
                s = sol_ref[cc, x - 1, :, lanes] + coef(0) * tile
                r = coef(8) * tile
                for k in range(1, S + 1):
                    tile = W[NW + k, cc, rows, :]
                    if k < S:
                        s = s + coef(k) * tile
                    r = r + coef(8 + k) * tile
                sol_ref[cc, x - 1, :, lanes] = s
                res_ref[cc, x - 1, :, lanes] = r
        return carry

    lax.fori_loop(1, NX + 1, final, 0)

    for v in list(range(NW)) + list(range(last + 1, NW + S)):
        for side in range(2):
            @pl.when(have[side])
            def _():
                for lt in range(2):
                    x_copy(v, side, lt).wait_send()

            @pl.when(have[2 + side])
            def _():
                y_copy(v, side).wait_send()

        for d in range(6):
            @pl.when(have[d])
            def _():
                e_copy(v, d).wait_send()

    for cyc in range(2):
        for k in range(ngz - 1):
            line_copy(cyc, k).wait_send()
        for k in range(ngx * ngy - 1):
            plane_copy(cyc, k).wait_send()


def solution(mesh):
    sizes = tuple(mesh.shape[a] for a in ("gx", "gy", "gz"))
    ngx, ngy, ngz = sizes

    def on_device(stencil, right_side):
        f32 = jnp.float32
        out = jax.ShapeDtypeStruct(right_side.shape, f32)
        dma = pltpu.SemaphoreType.DMA
        return pl.pallas_call(
            functools.partial(kernel, sizes),
            out_shape=(out, out),
            in_specs=[pl.BlockSpec(memory_space=pl.ANY)] * 2,
            out_specs=(pl.BlockSpec(memory_space=pltpu.VMEM),) * 2,
            scratch_shapes=[
                pltpu.VMEM(stencil.shape, stencil.dtype),
                pltpu.VMEM((NV, 2, 20 * PITCH + 8, LANES), f32),
                pltpu.VMEM((2, 4, 2, 32, LANES), f32),
                pltpu.VMEM((2, 4, 2, 8, LANES), f32),
                pltpu.VMEM((3, 2, 8, LANES), f32),
                pltpu.VMEM((NV, 2, 2, 2, 8, LANES), f32),
                pltpu.VMEM((NV, 2, 2, 2, 8, LANES), f32),
                pltpu.VMEM((NV, 6, 8, LANES), f32),
                pltpu.VMEM((NV, 8, LANES), f32),
                pltpu.VMEM((2, 16, 8, LANES), f32),
                pltpu.VMEM((2, ngz, 1, LANES), f32),
                pltpu.VMEM((2, ngx * ngy, 1, LANES), f32),
                pltpu.VMEM((2, 16, LANES), f32),
                pltpu.VMEM((40, LANES), f32),
                dma((17,)),
                dma((NV, 12)),
                dma((NV, 12)),
                dma((2, ngz - 1)),
                dma((2, ngz - 1)),
                dma((2, ngx * ngy - 1)),
                dma((2, ngx * ngy - 1)),
            ],
            compiler_params=pltpu.CompilerParams(
                collective_id=0, has_side_effects=True, vmem_limit_bytes=48 << 20
            ),
            name="gmres",
        )(
            pltpu.with_memory_space_constraint(stencil, pltpu.HBM),
            pltpu.with_memory_space_constraint(right_side, pltpu.HBM),
        )

    specs = (P(None, None, "gx", "gy", "gz"), P(None, "gx", "gy", "gz"))
    return jax.shard_map(
        on_device, mesh=mesh, in_specs=specs, out_specs=(specs[1], specs[1]), check_vma=False
    )
```

```python
import functools

import jax
import jax.numpy as jnp
from jax import lax
from jax.experimental import pallas as pl
from jax.experimental.pallas import tpu as pltpu
from jax.sharding import PartitionSpec as P

MESH = pl.DeviceIdType.MESH
S = 4
AHEAD = 3
shifts = (15.0, 2.0, 8.5, 4.75)
scale = 6.5
inv = 1.0 / scale

NW = S + 1 + AHEAD
NV = NW + S + 1
PITCH = 40
LANES = 128


def row(x, lt):
    return (2 * x + lt) * PITCH + 8


def kernel(
    sizes, st_hbm, rs_hbm, sol_ref, res_ref,
    st, W, xC, yC, eC, yh, ys, eh, eb, gacc, ar1, ar2, gB, cf,
    load_sem, near_sem, ssem, rsem, s1sem, r1sem, s2sem, r2sem,
):
    ngx, ngy, ngz = sizes
    gx, gy, gz = (lax.axis_index(a) for a in ("gx", "gy", "gz"))
    NX, NY = 8, 32
    have = (gx > 0, gx < ngx - 1, gy > 0, gy < ngy - 1, gz > 0, gz < ngz - 1)
    beside = (
        {"gx": lax.rem(gx + ngx - 1, ngx)}, {"gx": lax.rem(gx + 1, ngx)},
        {"gy": lax.rem(gy + ngy - 1, ngy)}, {"gy": lax.rem(gy + 1, ngy)},
        {"gz": lax.rem(gz + ngz - 1, ngz)}, {"gz": lax.rem(gz + 1, ngz)},
    )
    line = [{"gz": lax.rem(gz + k, ngz)} for k in range(1, ngz)]
    plane = [
        {"gx": lax.rem(gx + k // ngy, ngx), "gy": lax.rem(gy + k % ngy, ngy)}
        for k in range(1, ngx * ngy)
    ]
    lane = lax.broadcasted_iota(jnp.int32, (NY, LANES), 1)
    lane8 = lax.broadcasted_iota(jnp.int32, (8, LANES), 1)
    sub8 = lax.broadcasted_iota(jnp.int32, (8, LANES), 0)
    eye = lax.broadcasted_iota(jnp.int32, (16, LANES), 1) == lax.broadcasted_iota(jnp.int32, (16, LANES), 0)
    zero = jnp.zeros((NY, LANES), jnp.float32)

    loads = [pltpu.make_async_copy(st_hbm, st, load_sem.at[0])]
    for lt in range(2):
        for x in range(NX):
            loads.append(
                pltpu.make_async_copy(
                    rs_hbm.at[:, x, :, pl.ds(lt * LANES, LANES)],
                    W.at[0, :, pl.ds(row(x + 1, lt), NY), :],
                    load_sem.at[1 + lt * NX + x],
                )
            )
    for copy in loads[1:]:
        copy.start()
    loads[0].start()

    barrier = pltpu.get_barrier_semaphore()
    for peer in beside:
        pl.semaphore_signal(barrier, inc=1, device_id=peer, device_id_type=MESH)

    for v in range(NV):
        for c in range(2):
            for x in range(1, NX + 1):
                for lt in range(2):
                    W[v, c, pl.ds(row(x, lt) - 8, 8), :] = jnp.zeros((8, LANES), jnp.float32)
            W[v, c, pl.ds(row(NX + 1, 0) - 8, 8), :] = jnp.zeros((8, LANES), jnp.float32)
    for d in range(2):
        @pl.when(jnp.logical_not(have[d]))
        def _():
            for v in range(NV):
                for c in range(2):
                    for lt in range(2):
                        W[v, c, pl.ds(row(0 if d == 0 else NX + 1, lt), NY), :] = zero

        @pl.when(jnp.logical_not(have[2 + d]))
        def _():
            for v in range(NV):
                yh[v, d] = jnp.zeros((2, 2, NX, LANES), jnp.float32)

    for d in range(6):
        @pl.when(jnp.logical_not(have[d]))
        def _():
            for v in range(NV):
                eh[v, d] = jnp.zeros((8, LANES), jnp.float32)

    for cyc in range(2):
        gacc[cyc, 15] = jnp.zeros((8, LANES), jnp.float32)

    def tell(step):
        for peer in beside:
            pl.semaphore_signal(near_sem.at[step], inc=1, device_id=peer, device_id_type=MESH)

    def x_copy(v, side, lt):
        src = W.at[v, :, pl.ds(row(1 if side == 0 else NX, lt), NY), :]
        dst = W.at[v, :, pl.ds(row(NX + 1 if side == 0 else 0, lt), NY), :]
        k = 2 * side + lt
        return pltpu.make_async_remote_copy(
            src, dst, ssem.at[v, k], rsem.at[v, k], device_id=beside[side], device_id_type=MESH
        )

    def y_copy(v, side, lt):
        k = 10 + 2 * side + lt
        return pltpu.make_async_remote_copy(
            ys.at[v, side, lt], yh.at[v, 1 - side, lt], ssem.at[v, k], rsem.at[v, k],
            device_id=beside[2 + side], device_id_type=MESH,
        )

    def e_copy(v, d):
        return pltpu.make_async_remote_copy(
            eb.at[v], eh.at[v, d ^ 1], ssem.at[v, 4 + d], rsem.at[v, 4 + d],
            device_id=beside[d], device_id_type=MESH,
        )

    def send_x(v, side, lt):
        @pl.when(have[side])
        def _():
            x_copy(v, side, lt).start()

    def send_y(v, lt):
        for side in range(2):
            @pl.when(have[2 + side])
            def _():
                for c in range(2):
                    ys[v, side, lt, c] = W[
                        v, c, pl.ds(row(1, lt) + (0 if side == 0 else NY - 1), NX, stride=2 * PITCH), :
                    ]
                y_copy(v, side, lt).start()

    def send_edges(v):
        for d in range(6):
            @pl.when(have[d])
            def _():
                e_copy(v, d).start()

    def place_edge(packed, tile, side, t, c, x):
        n = side * 64 + t * 16 + c * 8 + x
        turn = n if side == 0 else (n + 1) % LANES
        tile = tile[8 * t:8 * t + 8]
        if turn:
            tile = pltpu.roll(tile, turn, 1)
        return jnp.where(lane8 == n, tile, packed)

    def pack_edges(v):
        packed = jnp.zeros((8, LANES), jnp.float32)
        for side in range(2):
            for c in range(2):
                for x in range(NX):
                    tile = W[v, c, pl.ds(row(x + 1, side), NY), :]
                    for t in range(4):
                        packed = place_edge(packed, tile, side, t, c, x)
        eb[v] = packed

    def unpack_edges(v, planes):
        packed = eb[v]
        for side in range(2):
            edge = 0 if side == 0 else LANES - 1
            for c in range(2):
                for x in planes:
                    for t in range(4):
                        turn = (edge - (side * 64 + t * 16 + c * 8 + x)) % LANES
                        moved = pltpu.roll(packed, turn, 1) if turn else packed
                        rows = pl.ds(row(x + 1, side) + 8 * t, 8)
                        W[v, c, rows, :] = jnp.where(lane8 == edge, moved, W[v, c, rows, :])

    def swapped(h):
        return jnp.where((lane8 & 8) == 0, pltpu.roll(h, LANES - 8, 1), pltpu.roll(h, 8, 1))

    def fix_edges(v):
        hz = pltpu.roll(jnp.where(lane8 < 64, eh[v, 5], eh[v, 4]), 64, 1)
        hy = jnp.where(
            sub8 == 0,
            pltpu.roll(pltpu.roll(eh[v, 2], LANES - 48, 1), 1, 0),
            pltpu.roll(pltpu.roll(eh[v, 3], 48, 1), 7, 0),
        )
        hx = jnp.where((lane8 & 7) == 0, pltpu.roll(eh[v, 0], LANES - 7, 1), pltpu.roll(eh[v, 1], 7, 1))
        part = eb[v + 1]
        for axis, h in enumerate((hx, hy, hz)):
            part = part + (eC[axis, 0] * h + eC[axis, 1] * swapped(h))
        eb[v + 1] = part

    def wait_halo(copy, side, axis):
        @pl.when(have[2 * axis + side])
        def _():
            copy.wait_recv()

    def wait_edges(v, d):
        @pl.when(have[d])
        def _():
            e_copy(v, d ^ 1).wait_recv()

    def interior_plane(v, x, left, right, shift):
        out = v + 1
        acc = [[None, None], [None, None]]

        def add(lt, p, b, src):
            for a in range(2):
                term = st[p, 2 * a + b, x - 1, :, lt * LANES:(lt + 1) * LANES].astype(jnp.float32) * src
                acc[lt][a] = term if acc[lt][a] is None else acc[lt][a] + term

        def at(b, xx, lt, off=0):
            start = row(xx, lt)
            if off == 0 and not isinstance(start, int):
                start = pl.multiple_of(start, 8)
            return W[v, b, pl.ds(start + off, NY), :]

        for b in range(2):
            centre = [at(b, x, lt) for lt in range(2)]
            up = [pltpu.roll(t, 1, 1) for t in centre]
            down = [pltpu.roll(t, LANES - 1, 1) for t in centre]
            for lt in range(2):
                add(lt, 0, b, centre[lt])
            add(0, 5, b, jnp.where(lane == 0, 0.0, up[0]))
            add(1, 5, b, jnp.where(lane == 0, up[0], up[1]))
            add(0, 6, b, jnp.where(lane == LANES - 1, down[1], down[0]))
            add(1, 6, b, jnp.where(lane == LANES - 1, 0.0, down[1]))
            for lt in range(2):
                if left:
                    add(lt, 1, b, at(b, x - 1, lt))
                if right:
                    add(lt, 2, b, at(b, x + 1, lt))
                add(lt, 3, b, at(b, x, lt, -1))
                add(lt, 4, b, at(b, x, lt, 1))
        for lt in range(2):
            for a in range(2):
                start = row(x, lt)
                if not isinstance(start, int):
                    start = pl.multiple_of(start, 8)
                W[out, a, pl.ds(start, NY), :] = (acc[lt][a] - shift * at(a, x, lt)) * inv

    def interior(v, shift):
        interior_plane(v, 1, False, True, shift)

        def body(x, carry):
            interior_plane(v, x, True, True, shift)
            return carry

        lax.fori_loop(2, NX, body, 0)
        interior_plane(v, NX, True, False, shift)
        pack_edges(v + 1)

    def fix_y(v, side, lt):
        out = v + 1
        h = [yh[v, side, lt, b] for b in range(2)]
        for a in range(2):
            part = yC[side, 2 * a, lt] * h[0] + yC[side, 2 * a + 1, lt] * h[1]
            rows = pl.ds(row(1, lt) + (0 if side == 0 else NY - 1), NX, stride=2 * PITCH)
            W[out, a, rows, :] = W[out, a, rows, :] + part

    def fix_x(v, side, lt):
        out = v + 1
        src = row(0 if side == 0 else NX + 1, lt)
        dst = pl.ds(row(1 if side == 0 else NX, lt), NY)
        h = [W[v, b, pl.ds(src, NY), :] for b in range(2)]
        for a in range(2):
            part = xC[side, 2 * a, lt] * h[0] + xC[side, 2 * a + 1, lt] * h[1]
            W[out, a, dst, :] = W[out, a, dst, :] + part

    def finish(v, sent, local):
        if not local:
            for d in range(6):
                wait_edges(v, d)
        fix_edges(v)
        if sent:
            send_edges(v + 1)
        unpack_edges(v + 1, (0, NX - 1))
        for lt in range(2):
            for side in range(2):
                @pl.when(have[2 + side])
                def _():
                    if not local:
                        y_copy(v, 1 - side, lt).wait_recv()
                    fix_y(v, side, lt)

            for side in range(2):
                @pl.when(have[side])
                def _():
                    if not local:
                        x_copy(v, 1 - side, lt).wait_recv()
                    fix_x(v, side, lt)
                    if sent:
                        x_copy(v + 1, side, lt).start()
            if sent:
                send_y(v + 1, lt)
        unpack_edges(v + 1, range(1, NX - 1))

    def drain(v):
        for d in range(6):
            @pl.when(have[d])
            def _():
                if d < 2:
                    for lt in range(2):
                        x_copy(v, d, lt).wait_send()
                elif d < 4:
                    for lt in range(2):
                        y_copy(v, d - 2, lt).wait_send()
                e_copy(v, d).wait_send()

    def gram_row(cyc, first, j):
        def body(x, accs):
            accs = list(accs)
            for c in range(2):
                for lt in range(2):
                    rows = pl.ds(pl.multiple_of(row(x, lt), 8), NY)
                    right = W[first + j, c, rows, :]
                    for i in range(j + 1):
                        left = right if i == j else W[first + i, c, rows, :]
                        accs[i] = accs[i] + jnp.sum((left * right).reshape(NY // 8, 8, LANES), axis=0)
            return tuple(accs)

        accs = lax.fori_loop(1, NX + 1, body, tuple(jnp.zeros((8, LANES), jnp.float32) for _ in range(j + 1)))
        for i in range(j + 1):
            gacc[cyc, j * (j + 1) // 2 + i] = accs[i]

    def line_copy(cyc, k):
        return pltpu.make_async_remote_copy(
            ar1.at[cyc, gz], ar1.at[cyc, gz], s1sem.at[cyc, k], r1sem.at[cyc, k],
            device_id=line[k], device_id_type=MESH,
        )

    def plane_copy(cyc, k):
        slot = gx * ngy + gy
        return pltpu.make_async_remote_copy(
            ar2.at[cyc, slot], ar2.at[cyc, slot], s2sem.at[cyc, k], r2sem.at[cyc, k],
            device_id=plane[k], device_id_type=MESH,
        )

    def reduce_start(cyc):
        rows = jnp.sum(jnp.sum(gacc[cyc], axis=1), axis=1, keepdims=True)
        ar1[cyc, gz] = jnp.sum(jnp.where(eye, rows, 0.0), axis=0, keepdims=True)
        for k in range(ngz - 1):
            line_copy(cyc, k).start()

    def reduce_middle(cyc):
        for k in range(ngz - 1):
            line_copy(cyc, k).wait_recv()
        ar2[cyc, gx * ngy + gy] = jnp.sum(ar1[cyc], axis=0)
        for k in range(ngx * ngy - 1):
            plane_copy(cyc, k).start()

    def reduce_end(cyc):
        for k in range(ngx * ngy - 1):
            plane_copy(cyc, k).wait_recv()
        total = jnp.sum(ar2[cyc], axis=0)
        rows = jnp.sum(jnp.where(eye, total, 0.0), axis=1, keepdims=True)
        gB[cyc] = jnp.broadcast_to(rows, (16, LANES))

    def solve(cyc):
        def G(i, j):
            i, j = min(i, j), max(i, j)
            return jnp.broadcast_to(gB[cyc, pl.ds(j * (j + 1) // 2 + i, 1), :], (8, LANES))

        g = [[G(i, j) for j in range(S + 1)] for i in range(S + 1)]
        gb = [[shifts[j] * g[i][j] + scale * g[i][j + 1] for j in range(S)] for i in range(S + 1)]
        h = [[shifts[i] * gb[i][j] + scale * gb[i + 1][j] if j <= i else None for j in range(S)] for i in range(S)]
        rhs = [gb[0][i] for i in range(S)]
        low = [[None] * S for _ in range(S)]
        dinv = [None] * S
        full = [[None] * S for _ in range(S)]
        for j in range(S):
            d = h[j][j]
            for k in range(j):
                d = d - low[j][k] * full[j][k]
            dinv[j] = 1.0 / d
            for i in range(j + 1, S):
                t = h[i][j]
                for k in range(j):
                    t = t - full[i][k] * low[j][k]
                full[i][j] = t
                low[i][j] = t * dinv[j]
        fwd = []
        for i in range(S):
            t = rhs[i]
            for k in range(i):
                t = t - low[i][k] * fwd[k]
            fwd.append(t)
        y = [None] * S
        for i in reversed(range(S)):
            t = fwd[i] * dinv[i]
            for k in range(i + 1, S):
                t = t - low[k][i] * y[k]
            y[i] = t
        c = []
        for j in range(S + 1):
            t = jnp.full((8, LANES), 1.0 if j == 0 else 0.0, jnp.float32)
            if j < S:
                t = t - shifts[j] * y[j]
            if j > 0:
                t = t - scale * y[j - 1]
            c.append(t)
        return y, c

    def put(n, value):
        cf[pl.ds(n, 1), :] = value[0:1]

    def coef(n):
        return cf[pl.ds(n, 1), :]

    for copy in loads[1:]:
        copy.wait()
    pack_edges(0)
    pl.semaphore_wait(barrier, 6)
    tell(0)
    send_edges(0)
    for lt in range(2):
        for side in range(2):
            send_x(0, side, lt)
        send_y(0, lt)
    loads[0].wait()

    def entry(p, e, x, lt):
        return st[p, e, x, :, lt * LANES:(lt + 1) * LANES].astype(jnp.float32) * inv

    for side in range(2):
        for e in range(4):
            for lt in range(2):
                edge = 0 if lt == 0 else LANES - 1
                xC[side, e, lt] = jnp.where(lane == edge, 0.0, entry(1 + side, e, 0 if side == 0 else NX - 1, lt))
                for x in range(NX):
                    part = st[3 + side, e, x, 16 * side:16 * side + 16, lt * LANES:(lt + 1) * LANES]
                    part = jnp.where(lane[:16] == edge, 0.0, part.astype(jnp.float32) * inv)
                    yC[side, e, lt, pl.ds(x, 1), :] = part[0:1] if side == 0 else part[15:16]
    for kind in range(2):
        ex, ey, ez = (jnp.zeros((8, LANES), jnp.float32),) * 3
        for side in range(2):
            for c in range(2):
                e = 3 * c if kind == 0 else c + 1
                for x in range(NX):
                    tile = entry(5 + side, e, x, side)
                    for t in range(4):
                        ez = place_edge(ez, tile, side, t, c, x)
                    ey = place_edge(ey, entry(3, e, x, side), side, 0, c, x)
                    ey = place_edge(ey, entry(4, e, x, side), side, 3, c, x)
                for p, x in ((1, 0), (2, NX - 1)):
                    tile = entry(p, e, x, side)
                    for t in range(4):
                        ex = place_edge(ex, tile, side, t, c, x)
        tile_y = (lane8 // 16) % 4
        inside = jnp.logical_or(
            jnp.logical_and(tile_y == 0, sub8 == 0), jnp.logical_and(tile_y == 3, sub8 == 7)
        )
        eC[0, kind] = ex
        eC[1, kind] = jnp.where(inside, ey, 0.0)
        eC[2, kind] = ez

    for j in range(S + AHEAD):
        interior(j, shifts[j % S])
        if j > 0:
            drain(j - 1)
        if j < 3:
            pl.semaphore_wait(near_sem.at[j], 6)
            if j < 2:
                tell(j + 1)
        if j < S:
            gram_row(0, 0, j)
        finish(j, True, False)
        if j + 1 == S:
            gram_row(0, 0, S)
            reduce_start(0)
        if j + 1 == S + 1:
            reduce_middle(0)
    if AHEAD == 0:
        reduce_middle(0)
    reduce_end(0)
    y, c = solve(0)
    for k in range(S):
        put(k, y[k])
    combo = [c + [None] * AHEAD]
    for j in range(AHEAD):
        old, new = combo[-1], []
        for k in range(NW):
            t = old[k - 1] if k > 0 else None
            factor = (shifts[k % S] - shifts[j]) * inv
            if old[k] is not None and factor != 0.0:
                t = factor * old[k] if t is None else t + factor * old[k]
            new.append(t)
        combo.append(new)
    place = {}
    for j in range(AHEAD + 1):
        for k in range(NW):
            if combo[j][k] is not None:
                place[j, k] = 8 + j * 8 + k
                put(place[j, k], combo[j][k])

    def combine(j, get):
        t = None
        for k in range(NW):
            if (j, k) in place:
                term = coef(place[j, k]) * get(k)
                t = term if t is None else t + term
        return t

    def second(x, carry):
        for cc in range(2):
            for lt in range(2):
                rows = pl.ds(pl.multiple_of(row(x, lt), 8), NY)
                tiles = [W[k, cc, rows, :] for k in range(NW)]
                for j in range(AHEAD + 1):
                    W[NW + j, cc, rows, :] = combine(j, lambda k: tiles[k])
        return carry

    lax.fori_loop(1, NX + 1, second, 0)
    last = NW + AHEAD
    interior(last, shifts[AHEAD])
    drain(NW - 2)
    for side in range(2):
        for lt in range(2):
            wait_halo(y_copy(NW - 1, 1 - side, lt), side, 1)
            wait_halo(x_copy(NW - 1, 1 - side, lt), side, 0)
    for d in range(6):
        wait_edges(NW - 1, d)
        eh[last, d] = combine(AHEAD, lambda k: eh[k, d])
    for side in range(2):
        for cc in range(2):
            for lt in range(2):
                rows = pl.ds(row(0 if side == 0 else NX + 1, lt), NY)
                W[last, cc, rows, :] = combine(AHEAD, lambda k: W[k, cc, rows, :])
                yh[last, side, lt, cc] = combine(AHEAD, lambda k: yh[k, side, lt, cc])
    finish(last, AHEAD + 1 < S, True)
    for j in range(AHEAD + 1):
        gram_row(1, NW, j)

    for j in range(AHEAD + 1, S):
        v = NW + j
        interior(v, shifts[j])
        gram_row(1, NW, j)
        finish(v, j + 1 < S, False)
    gram_row(1, NW, S)
    reduce_start(1)

    def first_share(x, carry):
        for cc in range(2):
            for lt in range(2):
                rows = pl.ds(pl.multiple_of(row(x, lt), 8), NY)
                t = coef(0) * W[0, cc, rows, :]
                for k in range(1, S):
                    t = t + coef(k) * W[k, cc, rows, :]
                sol_ref[cc, x - 1, :, lt * LANES:(lt + 1) * LANES] = t
        return carry

    lax.fori_loop(1, NX + 1, first_share, 0)
    drain(NW - 1)
    for v in range(last + 1, NW + S):
        drain(v)
    for k in range(ngz - 1):
        line_copy(0, k).wait_send()
    for k in range(ngx * ngy - 1):
        plane_copy(0, k).wait_send()
    reduce_middle(1)
    for k in range(ngz - 1):
        line_copy(1, k).wait_send()
    reduce_end(1)
    y, c = solve(1)
    for k in range(S):
        put(k, y[k])
    for k in range(S + 1):
        put(8 + k, c[k])

    def final(x, carry):
        for cc in range(2):
            for lt in range(2):
                rows = pl.ds(pl.multiple_of(row(x, lt), 8), NY)
                lanes = slice(lt * LANES, (lt + 1) * LANES)
                tile = W[NW, cc, rows, :]
                s = sol_ref[cc, x - 1, :, lanes] + coef(0) * tile
                r = coef(8) * tile
                for k in range(1, S + 1):
                    tile = W[NW + k, cc, rows, :]
                    if k < S:
                        s = s + coef(k) * tile
                    r = r + coef(8 + k) * tile
                sol_ref[cc, x - 1, :, lanes] = s
                res_ref[cc, x - 1, :, lanes] = r
        return carry

    lax.fori_loop(1, NX + 1, final, 0)
    for k in range(ngx * ngy - 1):
        plane_copy(1, k).wait_send()


def solution(mesh):
    sizes = tuple(mesh.shape[a] for a in ("gx", "gy", "gz"))
    ngx, ngy, ngz = sizes

    def on_device(stencil, right_side):
        f32 = jnp.float32
        out = jax.ShapeDtypeStruct(right_side.shape, f32)
        dma = pltpu.SemaphoreType.DMA
        return pl.pallas_call(
            functools.partial(kernel, sizes),
            out_shape=(out, out),
            in_specs=[pl.BlockSpec(memory_space=pl.ANY)] * 2,
            out_specs=(pl.BlockSpec(memory_space=pltpu.VMEM),) * 2,
            scratch_shapes=[
                pltpu.VMEM(stencil.shape, stencil.dtype),
                pltpu.VMEM((NV, 2, 20 * PITCH + 8, LANES), f32),
                pltpu.VMEM((2, 4, 2, 32, LANES), f32),
                pltpu.VMEM((2, 4, 2, 8, LANES), f32),
                pltpu.VMEM((3, 2, 8, LANES), f32),
                pltpu.VMEM((NV, 2, 2, 2, 8, LANES), f32),
                pltpu.VMEM((NV, 2, 2, 2, 8, LANES), f32),
                pltpu.VMEM((NV, 6, 8, LANES), f32),
                pltpu.VMEM((NV, 8, LANES), f32),
                pltpu.VMEM((2, 16, 8, LANES), f32),
                pltpu.VMEM((2, ngz, 1, LANES), f32),
                pltpu.VMEM((2, ngx * ngy, 1, LANES), f32),
                pltpu.VMEM((2, 16, LANES), f32),
                pltpu.VMEM((40, LANES), f32),
                dma((17,)),
                pltpu.SemaphoreType.REGULAR((3,)),
                dma((NV, 14)),
                dma((NV, 14)),
                dma((2, ngz - 1)),
                dma((2, ngz - 1)),
                dma((2, ngx * ngy - 1)),
                dma((2, ngx * ngy - 1)),
            ],
            compiler_params=pltpu.CompilerParams(
                collective_id=0, has_side_effects=True, vmem_limit_bytes=48 << 20
            ),
            name="gmres",
        )(
            pltpu.with_memory_space_constraint(stencil, pltpu.HBM),
            pltpu.with_memory_space_constraint(right_side, pltpu.HBM),
        )

    specs = (P(None, None, "gx", "gy", "gz"), P(None, "gx", "gy", "gz"))
    return jax.shard_map(
        on_device, mesh=mesh, in_specs=specs, out_specs=(specs[1], specs[1]), check_vma=False
    )
```

```python
import functools

import jax
import jax.numpy as jnp
from jax import lax
from jax.experimental import pallas as pl
from jax.experimental.pallas import tpu as pltpu
from jax.sharding import PartitionSpec as P

MESH = pl.DeviceIdType.MESH
S = 4
AHEAD = 3
shifts = (15.0, 2.0, 8.5, 4.75)
scale = 6.5
inv = 1.0 / scale

NW = S + 1 + AHEAD
NV = NW + S + 1
PITCH = 40
LANES = 128


def row(x, lt):
    return (2 * x + lt) * PITCH + 8


def kernel(
    sizes, st_hbm, rs_hbm, sol_ref, res_ref,
    st, W, xC, yC, eC, yh, ys, eh, eb, gacc, ar1, ar2, gB, cf,
    load_sem, near_sem, ssem, rsem, s1sem, r1sem, s2sem, r2sem,
):
    ngx, ngy, ngz = sizes
    gx, gy, gz = (lax.axis_index(a) for a in ("gx", "gy", "gz"))
    NX, NY = 8, 32
    have = (gx > 0, gx < ngx - 1, gy > 0, gy < ngy - 1, gz > 0, gz < ngz - 1)
    beside = (
        {"gx": lax.rem(gx + ngx - 1, ngx)}, {"gx": lax.rem(gx + 1, ngx)},
        {"gy": lax.rem(gy + ngy - 1, ngy)}, {"gy": lax.rem(gy + 1, ngy)},
        {"gz": lax.rem(gz + ngz - 1, ngz)}, {"gz": lax.rem(gz + 1, ngz)},
    )
    line = [{"gz": lax.rem(gz + k, ngz)} for k in range(1, ngz)]
    plane = [
        {"gx": lax.rem(gx + k // ngy, ngx), "gy": lax.rem(gy + k % ngy, ngy)}
        for k in range(1, ngx * ngy)
    ]
    lane = lax.broadcasted_iota(jnp.int32, (NY, LANES), 1)
    lane8 = lax.broadcasted_iota(jnp.int32, (8, LANES), 1)
    sub8 = lax.broadcasted_iota(jnp.int32, (8, LANES), 0)
    eye = lax.broadcasted_iota(jnp.int32, (16, LANES), 1) == lax.broadcasted_iota(jnp.int32, (16, LANES), 0)
    zero = jnp.zeros((NY, LANES), jnp.float32)

    loads = [pltpu.make_async_copy(st_hbm, st, load_sem.at[0])]
    for lt in range(2):
        for x in range(NX):
            loads.append(
                pltpu.make_async_copy(
                    rs_hbm.at[:, x, :, pl.ds(lt * LANES, LANES)],
                    W.at[0, :, pl.ds(row(x + 1, lt), NY), :],
                    load_sem.at[1 + lt * NX + x],
                )
            )
    for copy in loads[1:]:
        copy.start()
    loads[0].start()

    barrier = pltpu.get_barrier_semaphore()
    for peer in beside:
        pl.semaphore_signal(barrier, inc=1, device_id=peer, device_id_type=MESH)

    for v in range(NV):
        for c in range(2):
            for x in range(1, NX + 1):
                for lt in range(2):
                    W[v, c, pl.ds(row(x, lt) - 8, 8), :] = jnp.zeros((8, LANES), jnp.float32)
            W[v, c, pl.ds(row(NX + 1, 0) - 8, 8), :] = jnp.zeros((8, LANES), jnp.float32)
    for d in range(2):
        @pl.when(jnp.logical_not(have[d]))
        def _():
            for v in range(NV):
                for c in range(2):
                    for lt in range(2):
                        W[v, c, pl.ds(row(0 if d == 0 else NX + 1, lt), NY), :] = zero

        @pl.when(jnp.logical_not(have[2 + d]))
        def _():
            for v in range(NV):
                yh[v, d] = jnp.zeros((2, 2, NX, LANES), jnp.float32)

    for d in range(6):
        @pl.when(jnp.logical_not(have[d]))
        def _():
            for v in range(NV):
                eh[v, d] = jnp.zeros((8, LANES), jnp.float32)

    for cyc in range(2):
        gacc[cyc, 15] = jnp.zeros((8, LANES), jnp.float32)

    def tell(step):
        for peer in beside:
            pl.semaphore_signal(near_sem.at[step], inc=1, device_id=peer, device_id_type=MESH)

    def x_copy(v, side, lt):
        src = W.at[v, :, pl.ds(row(1 if side == 0 else NX, lt), NY), :]
        dst = W.at[v, :, pl.ds(row(NX + 1 if side == 0 else 0, lt), NY), :]
        k = 2 * side + lt
        return pltpu.make_async_remote_copy(
            src, dst, ssem.at[v, k], rsem.at[v, k], device_id=beside[side], device_id_type=MESH
        )

    def y_copy(v, side, lt):
        k = 10 + 2 * side + lt
        return pltpu.make_async_remote_copy(
            ys.at[v, side, lt], yh.at[v, 1 - side, lt], ssem.at[v, k], rsem.at[v, k],
            device_id=beside[2 + side], device_id_type=MESH,
        )

    def e_copy(v, d):
        return pltpu.make_async_remote_copy(
            eb.at[v], eh.at[v, d ^ 1], ssem.at[v, 4 + d], rsem.at[v, 4 + d],
            device_id=beside[d], device_id_type=MESH,
        )

    def send_x(v, side, lt):
        @pl.when(have[side])
        def _():
            x_copy(v, side, lt).start()

    def send_y(v, lt):
        for side in range(2):
            @pl.when(have[2 + side])
            def _():
                for c in range(2):
                    ys[v, side, lt, c] = W[
                        v, c, pl.ds(row(1, lt) + (0 if side == 0 else NY - 1), NX, stride=2 * PITCH), :
                    ]
                y_copy(v, side, lt).start()

    def send_edges(v):
        for d in range(6):
            @pl.when(have[d])
            def _():
                e_copy(v, d).start()

    def place_edge(packed, tile, side, t, c, x):
        n = side * 64 + t * 16 + c * 8 + x
        turn = n if side == 0 else (n + 1) % LANES
        tile = tile[8 * t:8 * t + 8]
        if turn:
            tile = pltpu.roll(tile, turn, 1)
        return jnp.where(lane8 == n, tile, packed)

    def pack_edges(v):
        packed = jnp.zeros((8, LANES), jnp.float32)
        for side in range(2):
            for c in range(2):
                for x in range(NX):
                    tile = W[v, c, pl.ds(row(x + 1, side), NY), :]
                    for t in range(4):
                        packed = place_edge(packed, tile, side, t, c, x)
        eb[v] = packed

    def unpack_edges(v, planes):
        packed = eb[v]
        for side in range(2):
            edge = 0 if side == 0 else LANES - 1
            for c in range(2):
                for x in planes:
                    for t in range(4):
                        turn = (edge - (side * 64 + t * 16 + c * 8 + x)) % LANES
                        moved = pltpu.roll(packed, turn, 1) if turn else packed
                        rows = pl.ds(row(x + 1, side) + 8 * t, 8)
                        W[v, c, rows, :] = jnp.where(lane8 == edge, moved, W[v, c, rows, :])

    def swapped(h):
        return jnp.where((lane8 & 8) == 0, pltpu.roll(h, LANES - 8, 1), pltpu.roll(h, 8, 1))

    def fix_edges(v):
        hz = pltpu.roll(jnp.where(lane8 < 64, eh[v, 5], eh[v, 4]), 64, 1)
        hy = jnp.where(
            sub8 == 0,
            pltpu.roll(pltpu.roll(eh[v, 2], LANES - 48, 1), 1, 0),
            pltpu.roll(pltpu.roll(eh[v, 3], 48, 1), 7, 0),
        )
        hx = jnp.where((lane8 & 7) == 0, pltpu.roll(eh[v, 0], LANES - 7, 1), pltpu.roll(eh[v, 1], 7, 1))
        part = eb[v + 1]
        for axis, h in enumerate((hx, hy, hz)):
            part = part + (eC[axis, 0] * h + eC[axis, 1] * swapped(h))
        eb[v + 1] = part

    def wait_halo(copy, side, axis):
        @pl.when(have[2 * axis + side])
        def _():
            copy.wait_recv()

    def wait_edges(v, d):
        @pl.when(have[d])
        def _():
            e_copy(v, d ^ 1).wait_recv()

    def interior_plane(v, x, left, right, shift):
        out = v + 1
        acc = [[None, None], [None, None]]

        def add(lt, p, b, src):
            for a in range(2):
                term = st[p, 2 * a + b, x - 1, :, lt * LANES:(lt + 1) * LANES].astype(jnp.float32) * src
                acc[lt][a] = term if acc[lt][a] is None else acc[lt][a] + term

        def at(b, xx, lt, off=0):
            start = row(xx, lt)
            if off == 0 and not isinstance(start, int):
                start = pl.multiple_of(start, 8)
            return W[v, b, pl.ds(start + off, NY), :]

        for b in range(2):
            centre = [at(b, x, lt) for lt in range(2)]
            up = [pltpu.roll(t, 1, 1) for t in centre]
            down = [pltpu.roll(t, LANES - 1, 1) for t in centre]
            for lt in range(2):
                add(lt, 0, b, centre[lt])
            add(0, 5, b, jnp.where(lane == 0, 0.0, up[0]))
            add(1, 5, b, jnp.where(lane == 0, up[0], up[1]))
            add(0, 6, b, jnp.where(lane == LANES - 1, down[1], down[0]))
            add(1, 6, b, jnp.where(lane == LANES - 1, 0.0, down[1]))
            for lt in range(2):
                if left:
                    add(lt, 1, b, at(b, x - 1, lt))
                if right:
                    add(lt, 2, b, at(b, x + 1, lt))
                add(lt, 3, b, at(b, x, lt, -1))
                add(lt, 4, b, at(b, x, lt, 1))
        for lt in range(2):
            for a in range(2):
                start = row(x, lt)
                if not isinstance(start, int):
                    start = pl.multiple_of(start, 8)
                W[out, a, pl.ds(start, NY), :] = (acc[lt][a] - shift * at(a, x, lt)) * inv

    def interior(v, shift):
        interior_plane(v, 1, False, True, shift)

        def body(x, carry):
            interior_plane(v, x, True, True, shift)
            return carry

        lax.fori_loop(2, NX, body, 0)
        interior_plane(v, NX, True, False, shift)
        pack_edges(v + 1)

    def fix_y(v, side, lt):
        out = v + 1
        h = [yh[v, side, lt, b] for b in range(2)]
        for a in range(2):
            part = yC[side, 2 * a, lt] * h[0] + yC[side, 2 * a + 1, lt] * h[1]
            rows = pl.ds(row(1, lt) + (0 if side == 0 else NY - 1), NX, stride=2 * PITCH)
            W[out, a, rows, :] = W[out, a, rows, :] + part

    def fix_x(v, side, lt):
        out = v + 1
        src = row(0 if side == 0 else NX + 1, lt)
        dst = pl.ds(row(1 if side == 0 else NX, lt), NY)
        h = [W[v, b, pl.ds(src, NY), :] for b in range(2)]
        for a in range(2):
            part = xC[side, 2 * a, lt] * h[0] + xC[side, 2 * a + 1, lt] * h[1]
            W[out, a, dst, :] = W[out, a, dst, :] + part

    def finish(v, sent, local):
        if not local:
            for d in range(6):
                wait_edges(v, d)
        fix_edges(v)
        if sent:
            send_edges(v + 1)
        unpack_edges(v + 1, (0, NX - 1))
        for lt in range(2):
            for side in range(2):
                @pl.when(have[2 + side])
                def _():
                    if not local:
                        y_copy(v, 1 - side, lt).wait_recv()
                    fix_y(v, side, lt)

            for side in range(2):
                @pl.when(have[side])
                def _():
                    if not local:
                        x_copy(v, 1 - side, lt).wait_recv()
                    fix_x(v, side, lt)
                    if sent:
                        x_copy(v + 1, side, lt).start()
            if sent:
                send_y(v + 1, lt)
        unpack_edges(v + 1, range(1, NX - 1))

    def drain(v):
        for d in range(6):
            @pl.when(have[d])
            def _():
                if d < 2:
                    for lt in range(2):
                        x_copy(v, d, lt).wait_send()
                elif d < 4:
                    for lt in range(2):
                        y_copy(v, d - 2, lt).wait_send()
                e_copy(v, d).wait_send()

    def gram_row(cyc, first, j):
        def body(x, accs):
            accs = list(accs)
            for c in range(2):
                for lt in range(2):
                    rows = pl.ds(pl.multiple_of(row(x, lt), 8), NY)
                    right = W[first + j, c, rows, :]
                    for i in range(j + 1):
                        left = right if i == j else W[first + i, c, rows, :]
                        accs[i] = accs[i] + jnp.sum((left * right).reshape(NY // 8, 8, LANES), axis=0)
            return tuple(accs)

        accs = lax.fori_loop(1, NX + 1, body, tuple(jnp.zeros((8, LANES), jnp.float32) for _ in range(j + 1)))
        for i in range(j + 1):
            gacc[cyc, j * (j + 1) // 2 + i] = accs[i]

    def line_copy(cyc, k):
        return pltpu.make_async_remote_copy(
            ar1.at[cyc, gz], ar1.at[cyc, gz], s1sem.at[cyc, k], r1sem.at[cyc, k],
            device_id=line[k], device_id_type=MESH,
        )

    def plane_copy(cyc, k):
        slot = gx * ngy + gy
        return pltpu.make_async_remote_copy(
            ar2.at[cyc, slot], ar2.at[cyc, slot], s2sem.at[cyc, k], r2sem.at[cyc, k],
            device_id=plane[k], device_id_type=MESH,
        )

    def reduce_start(cyc):
        rows = jnp.sum(jnp.sum(gacc[cyc], axis=1), axis=1, keepdims=True)
        ar1[cyc, gz] = jnp.sum(jnp.where(eye, rows, 0.0), axis=0, keepdims=True)
        for k in range(ngz - 1):
            line_copy(cyc, k).start()

    def reduce_middle(cyc):
        for k in range(ngz - 1):
            line_copy(cyc, k).wait_recv()
        ar2[cyc, gx * ngy + gy] = jnp.sum(ar1[cyc], axis=0)
        for k in range(ngx * ngy - 1):
            plane_copy(cyc, k).start()

    def reduce_end(cyc):
        for k in range(ngx * ngy - 1):
            plane_copy(cyc, k).wait_recv()
        total = jnp.sum(ar2[cyc], axis=0)
        rows = jnp.sum(jnp.where(eye, total, 0.0), axis=1, keepdims=True)
        gB[cyc] = jnp.broadcast_to(rows, (16, LANES))

    def solve(cyc):
        def G(i, j):
            i, j = min(i, j), max(i, j)
            return jnp.broadcast_to(gB[cyc, pl.ds(j * (j + 1) // 2 + i, 1), :], (8, LANES))

        g = [[G(i, j) for j in range(S + 1)] for i in range(S + 1)]
        gb = [[shifts[j] * g[i][j] + scale * g[i][j + 1] for j in range(S)] for i in range(S + 1)]
        h = [[shifts[i] * gb[i][j] + scale * gb[i + 1][j] if j <= i else None for j in range(S)] for i in range(S)]
        rhs = [gb[0][i] for i in range(S)]
        low = [[None] * S for _ in range(S)]
        dinv = [None] * S
        full = [[None] * S for _ in range(S)]
        for j in range(S):
            d = h[j][j]
            for k in range(j):
                d = d - low[j][k] * full[j][k]
            dinv[j] = 1.0 / d
            for i in range(j + 1, S):
                t = h[i][j]
                for k in range(j):
                    t = t - full[i][k] * low[j][k]
                full[i][j] = t
                low[i][j] = t * dinv[j]
        fwd = []
        for i in range(S):
            t = rhs[i]
            for k in range(i):
                t = t - low[i][k] * fwd[k]
            fwd.append(t)
        y = [None] * S
        for i in reversed(range(S)):
            t = fwd[i] * dinv[i]
            for k in range(i + 1, S):
                t = t - low[k][i] * y[k]
            y[i] = t
        c = []
        for j in range(S + 1):
            t = jnp.full((8, LANES), 1.0 if j == 0 else 0.0, jnp.float32)
            if j < S:
                t = t - shifts[j] * y[j]
            if j > 0:
                t = t - scale * y[j - 1]
            c.append(t)
        return y, c

    def put(n, value):
        cf[pl.ds(n, 1), :] = value[0:1]

    def coef(n):
        return cf[pl.ds(n, 1), :]

    for copy in loads[1:]:
        copy.wait()
    pack_edges(0)
    pl.semaphore_wait(barrier, 6)
    tell(0)
    send_edges(0)
    for lt in range(2):
        for side in range(2):
            send_x(0, side, lt)
        send_y(0, lt)
    loads[0].wait()

    def entry(p, e, x, lt):
        return st[p, e, x, :, lt * LANES:(lt + 1) * LANES].astype(jnp.float32) * inv

    for side in range(2):
        for e in range(4):
            for lt in range(2):
                edge = 0 if lt == 0 else LANES - 1
                xC[side, e, lt] = jnp.where(lane == edge, 0.0, entry(1 + side, e, 0 if side == 0 else NX - 1, lt))
                for x in range(NX):
                    part = st[3 + side, e, x, 16 * side:16 * side + 16, lt * LANES:(lt + 1) * LANES]
                    part = jnp.where(lane[:16] == edge, 0.0, part.astype(jnp.float32) * inv)
                    yC[side, e, lt, pl.ds(x, 1), :] = part[0:1] if side == 0 else part[15:16]
    for kind in range(2):
        ex, ey, ez = (jnp.zeros((8, LANES), jnp.float32),) * 3
        for side in range(2):
            for c in range(2):
                e = 3 * c if kind == 0 else c + 1
                for x in range(NX):
                    tile = entry(5 + side, e, x, side)
                    for t in range(4):
                        ez = place_edge(ez, tile, side, t, c, x)
                    ey = place_edge(ey, entry(3, e, x, side), side, 0, c, x)
                    ey = place_edge(ey, entry(4, e, x, side), side, 3, c, x)
                for p, x in ((1, 0), (2, NX - 1)):
                    tile = entry(p, e, x, side)
                    for t in range(4):
                        ex = place_edge(ex, tile, side, t, c, x)
        tile_y = (lane8 // 16) % 4
        inside = jnp.logical_or(
            jnp.logical_and(tile_y == 0, sub8 == 0), jnp.logical_and(tile_y == 3, sub8 == 7)
        )
        eC[0, kind] = ex
        eC[1, kind] = jnp.where(inside, ey, 0.0)
        eC[2, kind] = ez

    for j in range(S + AHEAD):
        interior(j, shifts[j % S])
        if j > 0:
            drain(j - 1)
        if j < 3:
            pl.semaphore_wait(near_sem.at[j], 6)
            if j < 2:
                tell(j + 1)
        if j < S:
            gram_row(0, 0, j)
        finish(j, True, False)
        if j + 1 == S:
            gram_row(0, 0, S)
            reduce_start(0)
        if j + 1 == S + 1:
            reduce_middle(0)
    if AHEAD == 0:
        reduce_middle(0)
    reduce_end(0)
    y, c = solve(0)
    for k in range(S):
        put(k, y[k])
    combo = [c + [None] * AHEAD]
    for j in range(AHEAD):
        old, new = combo[-1], []
        for k in range(NW):
            t = old[k - 1] if k > 0 else None
            factor = (shifts[k % S] - shifts[j]) * inv
            if old[k] is not None and factor != 0.0:
                t = factor * old[k] if t is None else t + factor * old[k]
            new.append(t)
        combo.append(new)
    place = {}
    for j in range(AHEAD + 1):
        for k in range(NW):
            if combo[j][k] is not None:
                place[j, k] = 8 + j * 8 + k
                put(place[j, k], combo[j][k])

    def combine(j, get):
        t = None
        for k in range(NW):
            if (j, k) in place:
                term = coef(place[j, k]) * get(k)
                t = term if t is None else t + term
        return t

    def second(x, carry):
        for cc in range(2):
            for lt in range(2):
                rows = pl.ds(pl.multiple_of(row(x, lt), 8), NY)
                tiles = [W[k, cc, rows, :] for k in range(NW)]
                for j in range(AHEAD + 1):
                    W[NW + j, cc, rows, :] = combine(j, lambda k: tiles[k])
        return carry

    lax.fori_loop(1, NX + 1, second, 0)
    last = NW + AHEAD
    interior(last, shifts[AHEAD])
    for j in range(AHEAD + 1):
        gram_row(1, NW, j)
    drain(NW - 2)
    for side in range(2):
        for lt in range(2):
            wait_halo(y_copy(NW - 1, 1 - side, lt), side, 1)
            wait_halo(x_copy(NW - 1, 1 - side, lt), side, 0)
    for d in range(6):
        wait_edges(NW - 1, d)
        eh[last, d] = combine(AHEAD, lambda k: eh[k, d])
    for side in range(2):
        for cc in range(2):
            for lt in range(2):
                rows = pl.ds(row(0 if side == 0 else NX + 1, lt), NY)
                W[last, cc, rows, :] = combine(AHEAD, lambda k: W[k, cc, rows, :])
                yh[last, side, lt, cc] = combine(AHEAD, lambda k: yh[k, side, lt, cc])
    finish(last, AHEAD + 1 < S, True)

    for j in range(AHEAD + 1, S):
        v = NW + j
        interior(v, shifts[j])
        gram_row(1, NW, j)
        finish(v, j + 1 < S, False)
    gram_row(1, NW, S)
    reduce_start(1)

    def first_share(x, carry):
        for cc in range(2):
            for lt in range(2):
                rows = pl.ds(pl.multiple_of(row(x, lt), 8), NY)
                t = coef(0) * W[0, cc, rows, :]
                for k in range(1, S):
                    t = t + coef(k) * W[k, cc, rows, :]
                sol_ref[cc, x - 1, :, lt * LANES:(lt + 1) * LANES] = t
        return carry

    lax.fori_loop(1, NX + 1, first_share, 0)
    drain(NW - 1)
    for v in range(last + 1, NW + S):
        drain(v)
    for k in range(ngz - 1):
        line_copy(0, k).wait_send()
    for k in range(ngx * ngy - 1):
        plane_copy(0, k).wait_send()
    reduce_middle(1)
    for k in range(ngz - 1):
        line_copy(1, k).wait_send()
    reduce_end(1)
    y, c = solve(1)
    for k in range(S):
        put(k, y[k])
    for k in range(S + 1):
        put(8 + k, c[k])

    def final(x, carry):
        for cc in range(2):
            for lt in range(2):
                rows = pl.ds(pl.multiple_of(row(x, lt), 8), NY)
                lanes = slice(lt * LANES, (lt + 1) * LANES)
                tile = W[NW, cc, rows, :]
                s = sol_ref[cc, x - 1, :, lanes] + coef(0) * tile
                r = coef(8) * tile
                for k in range(1, S + 1):
                    tile = W[NW + k, cc, rows, :]
                    if k < S:
                        s = s + coef(k) * tile
                    r = r + coef(8 + k) * tile
                sol_ref[cc, x - 1, :, lanes] = s
                res_ref[cc, x - 1, :, lanes] = r
        return carry

    lax.fori_loop(1, NX + 1, final, 0)
    for k in range(ngx * ngy - 1):
        plane_copy(1, k).wait_send()


def store(sol_ref, res_ref, sol_hbm, res_hbm, sem):
    copies = [
        pltpu.make_async_copy(src.at[c], dst.at[c], sem.at[i, c])
        for i, (src, dst) in enumerate(((sol_ref, sol_hbm), (res_ref, res_hbm)))
        for c in range(2)
    ]
    for copy in copies:
        copy.start()
    for copy in copies:
        copy.wait()


def solution(mesh):
    sizes = tuple(mesh.shape[a] for a in ("gx", "gy", "gz"))
    ngx, ngy, ngz = sizes

    def on_device(stencil, right_side):
        f32 = jnp.float32
        out = jax.ShapeDtypeStruct(right_side.shape, f32)
        dma = pltpu.SemaphoreType.DMA
        results = pl.pallas_call(
            functools.partial(kernel, sizes),
            out_shape=(out, out),
            in_specs=[pl.BlockSpec(memory_space=pl.ANY)] * 2,
            out_specs=(pl.BlockSpec(memory_space=pltpu.VMEM),) * 2,
            scratch_shapes=[
                pltpu.VMEM(stencil.shape, stencil.dtype),
                pltpu.VMEM((NV, 2, 20 * PITCH + 8, LANES), f32),
                pltpu.VMEM((2, 4, 2, 32, LANES), f32),
                pltpu.VMEM((2, 4, 2, 8, LANES), f32),
                pltpu.VMEM((3, 2, 8, LANES), f32),
                pltpu.VMEM((NV, 2, 2, 2, 8, LANES), f32),
                pltpu.VMEM((NV, 2, 2, 2, 8, LANES), f32),
                pltpu.VMEM((NV, 6, 8, LANES), f32),
                pltpu.VMEM((NV, 8, LANES), f32),
                pltpu.VMEM((2, 16, 8, LANES), f32),
                pltpu.VMEM((2, ngz, 1, LANES), f32),
                pltpu.VMEM((2, ngx * ngy, 1, LANES), f32),
                pltpu.VMEM((2, 16, LANES), f32),
                pltpu.VMEM((40, LANES), f32),
                dma((17,)),
                pltpu.SemaphoreType.REGULAR((3,)),
                dma((NV, 14)),
                dma((NV, 14)),
                dma((2, ngz - 1)),
                dma((2, ngz - 1)),
                dma((2, ngx * ngy - 1)),
                dma((2, ngx * ngy - 1)),
            ],
            compiler_params=pltpu.CompilerParams(
                collective_id=0, has_side_effects=True, vmem_limit_bytes=48 << 20
            ),
            name="gmres",
        )(
            pltpu.with_memory_space_constraint(stencil, pltpu.HBM),
            pltpu.with_memory_space_constraint(right_side, pltpu.HBM),
        )
        results = [pltpu.with_memory_space_constraint(r, pltpu.VMEM) for r in results]
        return pl.pallas_call(
            store,
            out_shape=(out, out),
            in_specs=[pl.BlockSpec(memory_space=pltpu.VMEM)] * 2,
            out_specs=(pl.BlockSpec(memory_space=pl.ANY),) * 2,
            scratch_shapes=[dma((2, 2))],
            compiler_params=pltpu.CompilerParams(vmem_limit_bytes=4 << 20),
            name="store",
        )(*results)

    specs = (P(None, None, "gx", "gy", "gz"), P(None, "gx", "gy", "gz"))
    return jax.shard_map(
        on_device, mesh=mesh, in_specs=specs, out_specs=(specs[1], specs[1]), check_vma=False
    )
```

```python
import functools

import jax
import jax.numpy as jnp
from jax import lax
from jax.experimental import pallas as pl
from jax.experimental.pallas import tpu as pltpu
from jax.sharding import PartitionSpec as P

MESH = pl.DeviceIdType.MESH
S = 4
AHEAD = S - 1
shifts = (15.0, 2.0, 8.5, 4.75)
scale = 6.5
inv = 1.0 / scale

NW = S + 1 + AHEAD
NV = NW + S + 1
PITCH = 40
LANES = 128


def row(x, lt):
    return (2 * x + lt) * PITCH + 8


def kernel(
    sizes, st_hbm, rs_hbm, sol_ref, res_ref,
    st, W, xC, yC, eC, yh, ys, eh, eb, gacc, ar1, ar2, gB, cf,
    load_sem, near_sem, ssem, rsem, s1sem, r1sem, s2sem, r2sem,
):
    ngx, ngy, ngz = sizes
    gx, gy, gz = (lax.axis_index(a) for a in ("gx", "gy", "gz"))
    NX, NY = 8, 32
    have = (gx > 0, gx < ngx - 1, gy > 0, gy < ngy - 1, gz > 0, gz < ngz - 1)
    beside = (
        {"gx": lax.rem(gx + ngx - 1, ngx)}, {"gx": lax.rem(gx + 1, ngx)},
        {"gy": lax.rem(gy + ngy - 1, ngy)}, {"gy": lax.rem(gy + 1, ngy)},
        {"gz": lax.rem(gz + ngz - 1, ngz)}, {"gz": lax.rem(gz + 1, ngz)},
    )
    line = [{"gz": lax.rem(gz + k, ngz)} for k in range(1, ngz)]
    plane = [
        {"gx": lax.rem(gx + k // ngy, ngx), "gy": lax.rem(gy + k % ngy, ngy)}
        for k in range(1, ngx * ngy)
    ]
    lane = lax.broadcasted_iota(jnp.int32, (NY, LANES), 1)
    lane8 = lax.broadcasted_iota(jnp.int32, (8, LANES), 1)
    sub8 = lax.broadcasted_iota(jnp.int32, (8, LANES), 0)
    eye = lax.broadcasted_iota(jnp.int32, (16, LANES), 1) == lax.broadcasted_iota(jnp.int32, (16, LANES), 0)
    zero = jnp.zeros((NY, LANES), jnp.float32)

    loads = [pltpu.make_async_copy(st_hbm, st, load_sem.at[0])]
    for lt in range(2):
        for x in range(NX):
            loads.append(
                pltpu.make_async_copy(
                    rs_hbm.at[:, x, :, pl.ds(lt * LANES, LANES)],
                    W.at[0, :, pl.ds(row(x + 1, lt), NY), :],
                    load_sem.at[1 + lt * NX + x],
                )
            )
    for copy in loads[1:]:
        copy.start()
    loads[0].start()

    barrier = pltpu.get_barrier_semaphore()
    for peer in beside:
        pl.semaphore_signal(barrier, inc=1, device_id=peer, device_id_type=MESH)

    for v in range(NV):
        for c in range(2):
            for x in range(1, NX + 1):
                for lt in range(2):
                    W[v, c, pl.ds(row(x, lt) - 8, 8), :] = jnp.zeros((8, LANES), jnp.float32)
            W[v, c, pl.ds(row(NX + 1, 0) - 8, 8), :] = jnp.zeros((8, LANES), jnp.float32)
    for d in range(2):
        @pl.when(jnp.logical_not(have[d]))
        def _():
            for v in range(NV):
                for c in range(2):
                    for lt in range(2):
                        W[v, c, pl.ds(row(0 if d == 0 else NX + 1, lt), NY), :] = zero

        @pl.when(jnp.logical_not(have[2 + d]))
        def _():
            for v in range(NV):
                yh[v, d] = jnp.zeros((2, 2, NX, LANES), jnp.float32)

    for d in range(6):
        @pl.when(jnp.logical_not(have[d]))
        def _():
            for v in range(NV):
                eh[v, d] = jnp.zeros((8, LANES), jnp.float32)

    for cyc in range(2):
        gacc[cyc, 15] = jnp.zeros((8, LANES), jnp.float32)

    def tell(step):
        for peer in beside:
            pl.semaphore_signal(near_sem.at[step], inc=1, device_id=peer, device_id_type=MESH)

    def x_copy(v, side, lt):
        src = W.at[v, :, pl.ds(row(1 if side == 0 else NX, lt), NY), :]
        dst = W.at[v, :, pl.ds(row(NX + 1 if side == 0 else 0, lt), NY), :]
        k = 2 * side + lt
        return pltpu.make_async_remote_copy(
            src, dst, ssem.at[v, k], rsem.at[v, k], device_id=beside[side], device_id_type=MESH
        )

    def y_copy(v, side, lt):
        k = 10 + 2 * side + lt
        return pltpu.make_async_remote_copy(
            ys.at[v, side, lt], yh.at[v, 1 - side, lt], ssem.at[v, k], rsem.at[v, k],
            device_id=beside[2 + side], device_id_type=MESH,
        )

    def e_copy(v, d):
        return pltpu.make_async_remote_copy(
            eb.at[v], eh.at[v, d ^ 1], ssem.at[v, 4 + d], rsem.at[v, 4 + d],
            device_id=beside[d], device_id_type=MESH,
        )

    def send_x(v, side, lt):
        @pl.when(have[side])
        def _():
            x_copy(v, side, lt).start()

    def send_y(v, lt):
        for side in range(2):
            @pl.when(have[2 + side])
            def _():
                for c in range(2):
                    ys[v, side, lt, c] = W[
                        v, c, pl.ds(row(1, lt) + (0 if side == 0 else NY - 1), NX, stride=2 * PITCH), :
                    ]
                y_copy(v, side, lt).start()

    def send_edges(v):
        for d in range(6):
            @pl.when(have[d])
            def _():
                e_copy(v, d).start()

    def place_edge(packed, tile, side, t, c, x):
        n = side * 64 + t * 16 + c * 8 + x
        turn = n if side == 0 else (n + 1) % LANES
        tile = tile[8 * t:8 * t + 8]
        if turn:
            tile = pltpu.roll(tile, turn, 1)
        return jnp.where(lane8 == n, tile, packed)

    def pack_edges(v):
        packed = jnp.zeros((8, LANES), jnp.float32)
        for side in range(2):
            for c in range(2):
                for x in range(NX):
                    tile = W[v, c, pl.ds(row(x + 1, side), NY), :]
                    for t in range(4):
                        packed = place_edge(packed, tile, side, t, c, x)
        eb[v] = packed

    def unpack_edges(v, planes):
        packed = eb[v]
        for side in range(2):
            edge = 0 if side == 0 else LANES - 1
            for c in range(2):
                for x in planes:
                    for t in range(4):
                        turn = (edge - (side * 64 + t * 16 + c * 8 + x)) % LANES
                        moved = pltpu.roll(packed, turn, 1) if turn else packed
                        rows = pl.ds(row(x + 1, side) + 8 * t, 8)
                        W[v, c, rows, :] = jnp.where(lane8 == edge, moved, W[v, c, rows, :])

    def swapped(h):
        return jnp.where((lane8 & 8) == 0, pltpu.roll(h, LANES - 8, 1), pltpu.roll(h, 8, 1))

    def fix_edges(v):
        hz = pltpu.roll(jnp.where(lane8 < 64, eh[v, 5], eh[v, 4]), 64, 1)
        hy = jnp.where(
            sub8 == 0,
            pltpu.roll(pltpu.roll(eh[v, 2], LANES - 48, 1), 1, 0),
            pltpu.roll(pltpu.roll(eh[v, 3], 48, 1), 7, 0),
        )
        hx = jnp.where((lane8 & 7) == 0, pltpu.roll(eh[v, 0], LANES - 7, 1), pltpu.roll(eh[v, 1], 7, 1))
        part = eb[v + 1]
        for axis, h in enumerate((hx, hy, hz)):
            part = part + (eC[axis, 0] * h + eC[axis, 1] * swapped(h))
        eb[v + 1] = part

    def wait_halo(copy, side, axis):
        @pl.when(have[2 * axis + side])
        def _():
            copy.wait_recv()

    def wait_edges(v, d):
        @pl.when(have[d])
        def _():
            e_copy(v, d ^ 1).wait_recv()

    def interior_plane(v, x, left, right, shift):
        out = v + 1
        acc = [[None, None], [None, None]]

        def add(lt, p, b, src):
            for a in range(2):
                term = st[p, 2 * a + b, x - 1, :, lt * LANES:(lt + 1) * LANES].astype(jnp.float32) * src
                acc[lt][a] = term if acc[lt][a] is None else acc[lt][a] + term

        def at(b, xx, lt, off=0):
            start = row(xx, lt)
            if off == 0 and not isinstance(start, int):
                start = pl.multiple_of(start, 8)
            return W[v, b, pl.ds(start + off, NY), :]

        for b in range(2):
            centre = [at(b, x, lt) for lt in range(2)]
            up = [pltpu.roll(t, 1, 1) for t in centre]
            down = [pltpu.roll(t, LANES - 1, 1) for t in centre]
            for lt in range(2):
                add(lt, 0, b, centre[lt])
            add(0, 5, b, jnp.where(lane == 0, 0.0, up[0]))
            add(1, 5, b, jnp.where(lane == 0, up[0], up[1]))
            add(0, 6, b, jnp.where(lane == LANES - 1, down[1], down[0]))
            add(1, 6, b, jnp.where(lane == LANES - 1, 0.0, down[1]))
            for lt in range(2):
                if left:
                    add(lt, 1, b, at(b, x - 1, lt))
                if right:
                    add(lt, 2, b, at(b, x + 1, lt))
                add(lt, 3, b, at(b, x, lt, -1))
                add(lt, 4, b, at(b, x, lt, 1))
        for lt in range(2):
            for a in range(2):
                start = row(x, lt)
                if not isinstance(start, int):
                    start = pl.multiple_of(start, 8)
                W[out, a, pl.ds(start, NY), :] = (acc[lt][a] - shift * at(a, x, lt)) * inv

    def interior(v, shift):
        interior_plane(v, 1, False, True, shift)

        def body(x, carry):
            interior_plane(v, x, True, True, shift)
            return carry

        lax.fori_loop(2, NX, body, 0)
        interior_plane(v, NX, True, False, shift)
        pack_edges(v + 1)

    def fix_y(v, side, lt):
        out = v + 1
        h = [yh[v, side, lt, b] for b in range(2)]
        for a in range(2):
            part = yC[side, 2 * a, lt] * h[0] + yC[side, 2 * a + 1, lt] * h[1]
            rows = pl.ds(row(1, lt) + (0 if side == 0 else NY - 1), NX, stride=2 * PITCH)
            W[out, a, rows, :] = W[out, a, rows, :] + part

    def fix_x(v, side, lt):
        out = v + 1
        src = row(0 if side == 0 else NX + 1, lt)
        dst = pl.ds(row(1 if side == 0 else NX, lt), NY)
        h = [W[v, b, pl.ds(src, NY), :] for b in range(2)]
        for a in range(2):
            part = xC[side, 2 * a, lt] * h[0] + xC[side, 2 * a + 1, lt] * h[1]
            W[out, a, dst, :] = W[out, a, dst, :] + part

    def finish(v, sent, local):
        if not local:
            for d in range(6):
                wait_edges(v, d)
        fix_edges(v)
        if sent:
            send_edges(v + 1)
        if sent:
            unpack_edges(v + 1, (0, NX - 1))
        for lt in range(2):
            for side in range(2):
                @pl.when(have[2 + side])
                def _():
                    if not local:
                        y_copy(v, 1 - side, lt).wait_recv()
                    fix_y(v, side, lt)

            for side in range(2):
                @pl.when(have[side])
                def _():
                    if not local:
                        x_copy(v, 1 - side, lt).wait_recv()
                    fix_x(v, side, lt)
                    if sent:
                        x_copy(v + 1, side, lt).start()
            if sent:
                send_y(v + 1, lt)
        if sent:
            unpack_edges(v + 1, range(1, NX - 1))

    def drain(v):
        for d in range(6):
            @pl.when(have[d])
            def _():
                if d < 2:
                    for lt in range(2):
                        x_copy(v, d, lt).wait_send()
                elif d < 4:
                    for lt in range(2):
                        y_copy(v, d - 2, lt).wait_send()
                e_copy(v, d).wait_send()

    def gram_row(cyc, first, j):
        def body(x, accs):
            accs = list(accs)
            for c in range(2):
                for lt in range(2):
                    rows = pl.ds(pl.multiple_of(row(x, lt), 8), NY)
                    right = W[first + j, c, rows, :]
                    for i in range(j + 1):
                        left = right if i == j else W[first + i, c, rows, :]
                        accs[i] = accs[i] + jnp.sum((left * right).reshape(NY // 8, 8, LANES), axis=0)
            return tuple(accs)

        accs = lax.fori_loop(1, NX + 1, body, tuple(jnp.zeros((8, LANES), jnp.float32) for _ in range(j + 1)))
        for i in range(j + 1):
            gacc[cyc, j * (j + 1) // 2 + i] = accs[i]

    def line_copy(cyc, k):
        return pltpu.make_async_remote_copy(
            ar1.at[cyc, gz], ar1.at[cyc, gz], s1sem.at[cyc, k], r1sem.at[cyc, k],
            device_id=line[k], device_id_type=MESH,
        )

    def plane_copy(cyc, k):
        slot = gx * ngy + gy
        return pltpu.make_async_remote_copy(
            ar2.at[cyc, slot], ar2.at[cyc, slot], s2sem.at[cyc, k], r2sem.at[cyc, k],
            device_id=plane[k], device_id_type=MESH,
        )

    def reduce_start(cyc):
        rows = jnp.sum(jnp.sum(gacc[cyc], axis=1), axis=1, keepdims=True)
        ar1[cyc, gz] = jnp.sum(jnp.where(eye, rows, 0.0), axis=0, keepdims=True)
        for k in range(ngz - 1):
            line_copy(cyc, k).start()

    def reduce_middle(cyc):
        for k in range(ngz - 1):
            line_copy(cyc, k).wait_recv()
        ar2[cyc, gx * ngy + gy] = jnp.sum(ar1[cyc], axis=0)
        for k in range(ngx * ngy - 1):
            plane_copy(cyc, k).start()

    def reduce_end(cyc):
        for k in range(ngx * ngy - 1):
            plane_copy(cyc, k).wait_recv()
        total = jnp.sum(ar2[cyc], axis=0)
        rows = jnp.sum(jnp.where(eye, total, 0.0), axis=1, keepdims=True)
        gB[cyc] = jnp.broadcast_to(rows, (16, LANES))

    def solve(cyc):
        def G(i, j):
            i, j = min(i, j), max(i, j)
            return jnp.broadcast_to(gB[cyc, pl.ds(j * (j + 1) // 2 + i, 1), :], (8, LANES))

        g = [[G(i, j) for j in range(S + 1)] for i in range(S + 1)]
        gb = [[shifts[j] * g[i][j] + scale * g[i][j + 1] for j in range(S)] for i in range(S + 1)]
        h = [[shifts[i] * gb[i][j] + scale * gb[i + 1][j] if j <= i else None for j in range(S)] for i in range(S)]
        rhs = [gb[0][i] for i in range(S)]
        low = [[None] * S for _ in range(S)]
        dinv = [None] * S
        full = [[None] * S for _ in range(S)]
        for j in range(S):
            d = h[j][j]
            for k in range(j):
                d = d - low[j][k] * full[j][k]
            dinv[j] = 1.0 / d
            for i in range(j + 1, S):
                t = h[i][j]
                for k in range(j):
                    t = t - full[i][k] * low[j][k]
                full[i][j] = t
                low[i][j] = t * dinv[j]
        fwd = []
        for i in range(S):
            t = rhs[i]
            for k in range(i):
                t = t - low[i][k] * fwd[k]
            fwd.append(t)
        y = [None] * S
        for i in reversed(range(S)):
            t = fwd[i] * dinv[i]
            for k in range(i + 1, S):
                t = t - low[k][i] * y[k]
            y[i] = t
        c = []
        for j in range(S + 1):
            t = jnp.full((8, LANES), 1.0 if j == 0 else 0.0, jnp.float32)
            if j < S:
                t = t - shifts[j] * y[j]
            if j > 0:
                t = t - scale * y[j - 1]
            c.append(t)
        return y, c

    def put(n, value):
        cf[pl.ds(n, 1), :] = value[0:1]

    def coef(n):
        return cf[pl.ds(n, 1), :]

    for copy in loads[1:]:
        copy.wait()
    pack_edges(0)
    pl.semaphore_wait(barrier, 6)
    tell(0)
    send_edges(0)
    for lt in range(2):
        for side in range(2):
            send_x(0, side, lt)
        send_y(0, lt)
    loads[0].wait()

    def entry(p, e, x, lt):
        return st[p, e, x, :, lt * LANES:(lt + 1) * LANES].astype(jnp.float32) * inv

    for side in range(2):
        for e in range(4):
            for lt in range(2):
                edge = 0 if lt == 0 else LANES - 1
                xC[side, e, lt] = jnp.where(lane == edge, 0.0, entry(1 + side, e, 0 if side == 0 else NX - 1, lt))
                for x in range(NX):
                    part = st[3 + side, e, x, 16 * side:16 * side + 16, lt * LANES:(lt + 1) * LANES]
                    part = jnp.where(lane[:16] == edge, 0.0, part.astype(jnp.float32) * inv)
                    yC[side, e, lt, pl.ds(x, 1), :] = part[0:1] if side == 0 else part[15:16]
    for kind in range(2):
        ex, ey, ez = (jnp.zeros((8, LANES), jnp.float32),) * 3
        for side in range(2):
            for c in range(2):
                e = 3 * c if kind == 0 else c + 1
                for x in range(NX):
                    tile = entry(5 + side, e, x, side)
                    for t in range(4):
                        ez = place_edge(ez, tile, side, t, c, x)
                    ey = place_edge(ey, entry(3, e, x, side), side, 0, c, x)
                    ey = place_edge(ey, entry(4, e, x, side), side, 3, c, x)
                for p, x in ((1, 0), (2, NX - 1)):
                    tile = entry(p, e, x, side)
                    for t in range(4):
                        ex = place_edge(ex, tile, side, t, c, x)
        tile_y = (lane8 // 16) % 4
        inside = jnp.logical_or(
            jnp.logical_and(tile_y == 0, sub8 == 0), jnp.logical_and(tile_y == 3, sub8 == 7)
        )
        eC[0, kind] = ex
        eC[1, kind] = jnp.where(inside, ey, 0.0)
        eC[2, kind] = ez

    for j in range(S + AHEAD):
        interior(j, shifts[j % S])
        if j > 0:
            drain(j - 1)
        if j < 3:
            pl.semaphore_wait(near_sem.at[j], 6)
            if j < 2:
                tell(j + 1)
        if j < S:
            gram_row(0, 0, j)
        finish(j, True, False)
        if j + 1 == S:
            gram_row(0, 0, S)
            reduce_start(0)
        if j + 1 == S + 1:
            reduce_middle(0)
    if AHEAD == 0:
        reduce_middle(0)
    reduce_end(0)
    y, c = solve(0)
    for k in range(S):
        put(k, y[k])
    combo = [c + [None] * AHEAD]
    for j in range(AHEAD):
        old, new = combo[-1], []
        for k in range(NW):
            t = old[k - 1] if k > 0 else None
            factor = (shifts[k % S] - shifts[j]) * inv
            if old[k] is not None and factor != 0.0:
                t = factor * old[k] if t is None else t + factor * old[k]
            new.append(t)
        combo.append(new)
    place = {}
    for j in range(AHEAD + 1):
        for k in range(NW):
            if combo[j][k] is not None:
                place[j, k] = 8 + j * 8 + k
                put(place[j, k], combo[j][k])

    def combine(j, get, ks=range(NW)):
        t = None
        for k in ks:
            if (j, k) in place:
                term = coef(place[j, k]) * get(k)
                t = term if t is None else t + term
        return t

    def second(x, carry):
        for cc in range(2):
            for lt in range(2):
                rows = pl.ds(pl.multiple_of(row(x, lt), 8), NY)
                tiles = [W[k, cc, rows, :] for k in range(NW)]
                for j in range(AHEAD + 1):
                    W[NW + j, cc, rows, :] = combine(j, lambda k: tiles[k])
        return carry

    lax.fori_loop(1, NX + 1, second, 0)
    for j in range(AHEAD + 1):
        eb[NW + j] = combine(j, lambda k: eb[k])
    last = NW + AHEAD
    interior(last, shifts[AHEAD])
    for j in range(AHEAD + 1):
        gram_row(1, NW, j)
    drain(NW - 2)
    early = range(NW - 1)
    end = coef(place[AHEAD, NW - 1])
    for side in range(2):
        for cc in range(2):
            for lt in range(2):
                rows = pl.ds(row(0 if side == 0 else NX + 1, lt), NY)
                W[last, cc, rows, :] = combine(AHEAD, lambda k: W[k, cc, rows, :], early)
                yh[last, side, lt, cc] = combine(AHEAD, lambda k: yh[k, side, lt, cc], early)
    for d in range(6):
        eh[last, d] = combine(AHEAD, lambda k: eh[k, d], early)
    for side in range(2):
        for lt in range(2):
            wait_halo(y_copy(NW - 1, 1 - side, lt), side, 1)
            wait_halo(x_copy(NW - 1, 1 - side, lt), side, 0)
    for d in range(6):
        wait_edges(NW - 1, d)
        eh[last, d] = eh[last, d] + end * eh[NW - 1, d]
    for side in range(2):
        for cc in range(2):
            for lt in range(2):
                rows = pl.ds(row(0 if side == 0 else NX + 1, lt), NY)
                W[last, cc, rows, :] = W[last, cc, rows, :] + end * W[NW - 1, cc, rows, :]
                yh[last, side, lt, cc] = yh[last, side, lt, cc] + end * yh[NW - 1, side, lt, cc]
    edges_before = eb[last + 1]
    finish(last, False, True)

    gram_row(1, NW, S)
    edges = eb[last + 1]
    base = S * (S + 1) // 2
    for i in range(S):
        gacc[1, base + i] = gacc[1, base + i] + eb[NW + i] * (edges - edges_before)
    gacc[1, base + S] = gacc[1, base + S] + (edges * edges - edges_before * edges_before)
    reduce_start(1)
    unpack_edges(last + 1, range(NX))

    def first_share(x, carry):
        for cc in range(2):
            for lt in range(2):
                rows = pl.ds(pl.multiple_of(row(x, lt), 8), NY)
                t = coef(0) * W[0, cc, rows, :]
                for k in range(1, S):
                    t = t + coef(k) * W[k, cc, rows, :]
                sol_ref[cc, x - 1, :, lt * LANES:(lt + 1) * LANES] = t
        return carry

    lax.fori_loop(1, NX + 1, first_share, 0)
    drain(NW - 1)
    for v in range(last + 1, NW + S):
        drain(v)
    for k in range(ngz - 1):
        line_copy(0, k).wait_send()
    for k in range(ngx * ngy - 1):
        plane_copy(0, k).wait_send()
    reduce_middle(1)
    for k in range(ngz - 1):
        line_copy(1, k).wait_send()
    reduce_end(1)
    y, c = solve(1)
    for k in range(S):
        put(k, y[k])
    for k in range(S + 1):
        put(8 + k, c[k])

    def final(x, carry):
        for cc in range(2):
            for lt in range(2):
                rows = pl.ds(pl.multiple_of(row(x, lt), 8), NY)
                lanes = slice(lt * LANES, (lt + 1) * LANES)
                tile = W[NW, cc, rows, :]
                s = sol_ref[cc, x - 1, :, lanes] + coef(0) * tile
                r = coef(8) * tile
                for k in range(1, S + 1):
                    tile = W[NW + k, cc, rows, :]
                    if k < S:
                        s = s + coef(k) * tile
                    r = r + coef(8 + k) * tile
                sol_ref[cc, x - 1, :, lanes] = s
                res_ref[cc, x - 1, :, lanes] = r
        return carry

    lax.fori_loop(1, NX + 1, final, 0)
    for k in range(ngx * ngy - 1):
        plane_copy(1, k).wait_send()


def store(sol_ref, res_ref, sol_hbm, res_hbm, sem):
    copies = [
        pltpu.make_async_copy(src.at[c], dst.at[c], sem.at[i, c])
        for i, (src, dst) in enumerate(((sol_ref, sol_hbm), (res_ref, res_hbm)))
        for c in range(2)
    ]
    for copy in copies:
        copy.start()
    for copy in copies:
        copy.wait()


def solution(mesh):
    sizes = tuple(mesh.shape[a] for a in ("gx", "gy", "gz"))
    ngx, ngy, ngz = sizes

    def on_device(stencil, right_side):
        f32 = jnp.float32
        out = jax.ShapeDtypeStruct(right_side.shape, f32)
        dma = pltpu.SemaphoreType.DMA
        results = pl.pallas_call(
            functools.partial(kernel, sizes),
            out_shape=(out, out),
            in_specs=[pl.BlockSpec(memory_space=pl.ANY)] * 2,
            out_specs=(pl.BlockSpec(memory_space=pltpu.VMEM),) * 2,
            scratch_shapes=[
                pltpu.VMEM(stencil.shape, stencil.dtype),
                pltpu.VMEM((NV, 2, 20 * PITCH + 8, LANES), f32),
                pltpu.VMEM((2, 4, 2, 32, LANES), f32),
                pltpu.VMEM((2, 4, 2, 8, LANES), f32),
                pltpu.VMEM((3, 2, 8, LANES), f32),
                pltpu.VMEM((NV, 2, 2, 2, 8, LANES), f32),
                pltpu.VMEM((NV, 2, 2, 2, 8, LANES), f32),
                pltpu.VMEM((NV, 6, 8, LANES), f32),
                pltpu.VMEM((NV, 8, LANES), f32),
                pltpu.VMEM((2, 16, 8, LANES), f32),
                pltpu.VMEM((2, ngz, 1, LANES), f32),
                pltpu.VMEM((2, ngx * ngy, 1, LANES), f32),
                pltpu.VMEM((2, 16, LANES), f32),
                pltpu.VMEM((40, LANES), f32),
                dma((17,)),
                pltpu.SemaphoreType.REGULAR((3,)),
                dma((NV, 14)),
                dma((NV, 14)),
                dma((2, ngz - 1)),
                dma((2, ngz - 1)),
                dma((2, ngx * ngy - 1)),
                dma((2, ngx * ngy - 1)),
            ],
            compiler_params=pltpu.CompilerParams(
                collective_id=0, has_side_effects=True, vmem_limit_bytes=48 << 20
            ),
            name="gmres",
        )(
            pltpu.with_memory_space_constraint(stencil, pltpu.HBM),
            pltpu.with_memory_space_constraint(right_side, pltpu.HBM),
        )
        results = [pltpu.with_memory_space_constraint(r, pltpu.VMEM) for r in results]
        return pl.pallas_call(
            store,
            out_shape=(out, out),
            in_specs=[pl.BlockSpec(memory_space=pltpu.VMEM)] * 2,
            out_specs=(pl.BlockSpec(memory_space=pl.ANY),) * 2,
            scratch_shapes=[dma((2, 2))],
            compiler_params=pltpu.CompilerParams(vmem_limit_bytes=4 << 20),
            name="store",
        )(*results)

    specs = (P(None, None, "gx", "gy", "gz"), P(None, "gx", "gy", "gz"))
    return jax.shard_map(
        on_device, mesh=mesh, in_specs=specs, out_specs=(specs[1], specs[1]), check_vma=False
    )
```

```python
import functools

import jax
import jax.numpy as jnp
from jax import lax
from jax.experimental import pallas as pl
from jax.experimental.pallas import tpu as pltpu
from jax.sharding import PartitionSpec as P

MESH = pl.DeviceIdType.MESH
S = 4
AHEAD = S - 1
shifts = (15.0, 2.0, 8.5, 4.75)
scale = 6.5
inv = 1.0 / scale

NW = S + 1 + AHEAD
NV = NW + S + 1
PITCH = 40
LANES = 128


def row(x, lt):
    return (2 * x + lt) * PITCH + 8


def kernel(
    sizes, st_hbm, rs_hbm, first_ref, basis_ref, weights_ref,
    st, W, xC, yC, eC, yh, ys, eh, eb, gacc, ar1, ar2, gB, cf,
    load_sem, near_sem, ssem, rsem, s1sem, r1sem, s2sem, r2sem,
):
    ngx, ngy, ngz = sizes
    gx, gy, gz = (lax.axis_index(a) for a in ("gx", "gy", "gz"))
    NX, NY = 8, 32
    have = (gx > 0, gx < ngx - 1, gy > 0, gy < ngy - 1, gz > 0, gz < ngz - 1)
    beside = (
        {"gx": lax.rem(gx + ngx - 1, ngx)}, {"gx": lax.rem(gx + 1, ngx)},
        {"gy": lax.rem(gy + ngy - 1, ngy)}, {"gy": lax.rem(gy + 1, ngy)},
        {"gz": lax.rem(gz + ngz - 1, ngz)}, {"gz": lax.rem(gz + 1, ngz)},
    )
    line = [{"gz": lax.rem(gz + k, ngz)} for k in range(1, ngz)]
    plane = [
        {"gx": lax.rem(gx + k // ngy, ngx), "gy": lax.rem(gy + k % ngy, ngy)}
        for k in range(1, ngx * ngy)
    ]
    lane = lax.broadcasted_iota(jnp.int32, (NY, LANES), 1)
    lane8 = lax.broadcasted_iota(jnp.int32, (8, LANES), 1)
    sub8 = lax.broadcasted_iota(jnp.int32, (8, LANES), 0)
    eye = lax.broadcasted_iota(jnp.int32, (16, LANES), 1) == lax.broadcasted_iota(jnp.int32, (16, LANES), 0)
    zero = jnp.zeros((NY, LANES), jnp.float32)

    loads = [pltpu.make_async_copy(st_hbm, st, load_sem.at[0])]
    for lt in range(2):
        for x in range(NX):
            loads.append(
                pltpu.make_async_copy(
                    rs_hbm.at[:, x, :, pl.ds(lt * LANES, LANES)],
                    W.at[0, :, pl.ds(row(x + 1, lt), NY), :],
                    load_sem.at[1 + lt * NX + x],
                )
            )
    for copy in loads[1:]:
        copy.start()
    loads[0].start()

    barrier = pltpu.get_barrier_semaphore()
    for peer in beside:
        pl.semaphore_signal(barrier, inc=1, device_id=peer, device_id_type=MESH)

    for v in range(NV):
        for c in range(2):
            for x in range(1, NX + 1):
                for lt in range(2):
                    W[v, c, pl.ds(row(x, lt) - 8, 8), :] = jnp.zeros((8, LANES), jnp.float32)
            W[v, c, pl.ds(row(NX + 1, 0) - 8, 8), :] = jnp.zeros((8, LANES), jnp.float32)
    for d in range(2):
        @pl.when(jnp.logical_not(have[d]))
        def _():
            for v in range(NV):
                for c in range(2):
                    for lt in range(2):
                        W[v, c, pl.ds(row(0 if d == 0 else NX + 1, lt), NY), :] = zero

        @pl.when(jnp.logical_not(have[2 + d]))
        def _():
            for v in range(NV):
                yh[v, d] = jnp.zeros((2, 2, NX, LANES), jnp.float32)

    for d in range(6):
        @pl.when(jnp.logical_not(have[d]))
        def _():
            for v in range(NV):
                eh[v, d] = jnp.zeros((8, LANES), jnp.float32)

    for cyc in range(2):
        gacc[cyc, 15] = jnp.zeros((8, LANES), jnp.float32)

    def tell(step):
        for peer in beside:
            pl.semaphore_signal(near_sem.at[step], inc=1, device_id=peer, device_id_type=MESH)

    def x_copy(v, side, lt):
        src = W.at[v, :, pl.ds(row(1 if side == 0 else NX, lt), NY), :]
        dst = W.at[v, :, pl.ds(row(NX + 1 if side == 0 else 0, lt), NY), :]
        k = 2 * side + lt
        return pltpu.make_async_remote_copy(
            src, dst, ssem.at[v, k], rsem.at[v, k], device_id=beside[side], device_id_type=MESH
        )

    def y_copy(v, side, lt):
        k = 10 + 2 * side + lt
        return pltpu.make_async_remote_copy(
            ys.at[v, side, lt], yh.at[v, 1 - side, lt], ssem.at[v, k], rsem.at[v, k],
            device_id=beside[2 + side], device_id_type=MESH,
        )

    def e_copy(v, d):
        return pltpu.make_async_remote_copy(
            eb.at[v], eh.at[v, d ^ 1], ssem.at[v, 4 + d], rsem.at[v, 4 + d],
            device_id=beside[d], device_id_type=MESH,
        )

    def send_x(v, side, lt):
        @pl.when(have[side])
        def _():
            x_copy(v, side, lt).start()

    def send_y(v, lt):
        for side in range(2):
            @pl.when(have[2 + side])
            def _():
                for c in range(2):
                    ys[v, side, lt, c] = W[
                        v, c, pl.ds(row(1, lt) + (0 if side == 0 else NY - 1), NX, stride=2 * PITCH), :
                    ]
                y_copy(v, side, lt).start()

    def send_edges(v):
        for d in range(6):
            @pl.when(have[d])
            def _():
                e_copy(v, d).start()

    def place_edge(packed, tile, side, t, c, x):
        n = side * 64 + t * 16 + c * 8 + x
        turn = n if side == 0 else (n + 1) % LANES
        tile = tile[8 * t:8 * t + 8]
        if turn:
            tile = pltpu.roll(tile, turn, 1)
        return jnp.where(lane8 == n, tile, packed)

    def pack_edges(v):
        packed = jnp.zeros((8, LANES), jnp.float32)
        for side in range(2):
            for c in range(2):
                for x in range(NX):
                    tile = W[v, c, pl.ds(row(x + 1, side), NY), :]
                    for t in range(4):
                        packed = place_edge(packed, tile, side, t, c, x)
        eb[v] = packed

    def unpack_edges(v, planes):
        packed = eb[v]
        for side in range(2):
            edge = 0 if side == 0 else LANES - 1
            for c in range(2):
                for x in planes:
                    for t in range(4):
                        turn = (edge - (side * 64 + t * 16 + c * 8 + x)) % LANES
                        moved = pltpu.roll(packed, turn, 1) if turn else packed
                        rows = pl.ds(row(x + 1, side) + 8 * t, 8)
                        W[v, c, rows, :] = jnp.where(lane8 == edge, moved, W[v, c, rows, :])

    def swapped(h):
        return jnp.where((lane8 & 8) == 0, pltpu.roll(h, LANES - 8, 1), pltpu.roll(h, 8, 1))

    def fix_edges(v):
        hz = pltpu.roll(jnp.where(lane8 < 64, eh[v, 5], eh[v, 4]), 64, 1)
        hy = jnp.where(
            sub8 == 0,
            pltpu.roll(pltpu.roll(eh[v, 2], LANES - 48, 1), 1, 0),
            pltpu.roll(pltpu.roll(eh[v, 3], 48, 1), 7, 0),
        )
        hx = jnp.where((lane8 & 7) == 0, pltpu.roll(eh[v, 0], LANES - 7, 1), pltpu.roll(eh[v, 1], 7, 1))
        part = eb[v + 1]
        for axis, h in enumerate((hx, hy, hz)):
            part = part + (eC[axis, 0] * h + eC[axis, 1] * swapped(h))
        eb[v + 1] = part

    def wait_halo(copy, side, axis):
        @pl.when(have[2 * axis + side])
        def _():
            copy.wait_recv()

    def wait_edges(v, d):
        @pl.when(have[d])
        def _():
            e_copy(v, d ^ 1).wait_recv()

    def interior_plane(v, x, left, right, shift):
        out = v + 1
        acc = [[None, None], [None, None]]

        def add(lt, p, b, src):
            for a in range(2):
                term = st[p, 2 * a + b, x - 1, :, lt * LANES:(lt + 1) * LANES].astype(jnp.float32) * src
                acc[lt][a] = term if acc[lt][a] is None else acc[lt][a] + term

        def at(b, xx, lt, off=0):
            start = row(xx, lt)
            if off == 0 and not isinstance(start, int):
                start = pl.multiple_of(start, 8)
            return W[v, b, pl.ds(start + off, NY), :]

        for b in range(2):
            centre = [at(b, x, lt) for lt in range(2)]
            up = [pltpu.roll(t, 1, 1) for t in centre]
            down = [pltpu.roll(t, LANES - 1, 1) for t in centre]
            for lt in range(2):
                add(lt, 0, b, centre[lt])
            add(0, 5, b, jnp.where(lane == 0, 0.0, up[0]))
            add(1, 5, b, jnp.where(lane == 0, up[0], up[1]))
            add(0, 6, b, jnp.where(lane == LANES - 1, down[1], down[0]))
            add(1, 6, b, jnp.where(lane == LANES - 1, 0.0, down[1]))
            for lt in range(2):
                if left:
                    add(lt, 1, b, at(b, x - 1, lt))
                if right:
                    add(lt, 2, b, at(b, x + 1, lt))
                add(lt, 3, b, at(b, x, lt, -1))
                add(lt, 4, b, at(b, x, lt, 1))
        for lt in range(2):
            for a in range(2):
                start = row(x, lt)
                if not isinstance(start, int):
                    start = pl.multiple_of(start, 8)
                W[out, a, pl.ds(start, NY), :] = (acc[lt][a] - shift * at(a, x, lt)) * inv

    def interior(v, shift):
        interior_plane(v, 1, False, True, shift)

        def body(x, carry):
            interior_plane(v, x, True, True, shift)
            return carry

        lax.fori_loop(2, NX, body, 0)
        interior_plane(v, NX, True, False, shift)
        pack_edges(v + 1)

    def fix_y(v, side, lt):
        out = v + 1
        h = [yh[v, side, lt, b] for b in range(2)]
        for a in range(2):
            part = yC[side, 2 * a, lt] * h[0] + yC[side, 2 * a + 1, lt] * h[1]
            rows = pl.ds(row(1, lt) + (0 if side == 0 else NY - 1), NX, stride=2 * PITCH)
            W[out, a, rows, :] = W[out, a, rows, :] + part

    def fix_x(v, side, lt):
        out = v + 1
        src = row(0 if side == 0 else NX + 1, lt)
        dst = pl.ds(row(1 if side == 0 else NX, lt), NY)
        h = [W[v, b, pl.ds(src, NY), :] for b in range(2)]
        for a in range(2):
            part = xC[side, 2 * a, lt] * h[0] + xC[side, 2 * a + 1, lt] * h[1]
            W[out, a, dst, :] = W[out, a, dst, :] + part

    def finish(v, sent, local):
        if not local:
            for d in range(6):
                wait_edges(v, d)
        fix_edges(v)
        if sent:
            send_edges(v + 1)
        if sent:
            unpack_edges(v + 1, (0, NX - 1))
        for lt in range(2):
            for side in range(2):
                @pl.when(have[2 + side])
                def _():
                    if not local:
                        y_copy(v, 1 - side, lt).wait_recv()
                    fix_y(v, side, lt)

            for side in range(2):
                @pl.when(have[side])
                def _():
                    if not local:
                        x_copy(v, 1 - side, lt).wait_recv()
                    fix_x(v, side, lt)
                    if sent:
                        x_copy(v + 1, side, lt).start()
            if sent:
                send_y(v + 1, lt)
        if sent:
            unpack_edges(v + 1, range(1, NX - 1))

    def drain(v):
        for d in range(6):
            @pl.when(have[d])
            def _():
                if d < 2:
                    for lt in range(2):
                        x_copy(v, d, lt).wait_send()
                elif d < 4:
                    for lt in range(2):
                        y_copy(v, d - 2, lt).wait_send()
                e_copy(v, d).wait_send()

    def gram_row(cyc, first, j):
        def body(x, accs):
            accs = list(accs)
            for c in range(2):
                for lt in range(2):
                    rows = pl.ds(pl.multiple_of(row(x, lt), 8), NY)
                    right = W[first + j, c, rows, :]
                    for i in range(j + 1):
                        left = right if i == j else W[first + i, c, rows, :]
                        accs[i] = accs[i] + jnp.sum((left * right).reshape(NY // 8, 8, LANES), axis=0)
            return tuple(accs)

        accs = lax.fori_loop(1, NX + 1, body, tuple(jnp.zeros((8, LANES), jnp.float32) for _ in range(j + 1)))
        for i in range(j + 1):
            gacc[cyc, j * (j + 1) // 2 + i] = accs[i]

    def line_copy(cyc, k):
        return pltpu.make_async_remote_copy(
            ar1.at[cyc, gz], ar1.at[cyc, gz], s1sem.at[cyc, k], r1sem.at[cyc, k],
            device_id=line[k], device_id_type=MESH,
        )

    def plane_copy(cyc, k):
        slot = gx * ngy + gy
        return pltpu.make_async_remote_copy(
            ar2.at[cyc, slot], ar2.at[cyc, slot], s2sem.at[cyc, k], r2sem.at[cyc, k],
            device_id=plane[k], device_id_type=MESH,
        )

    def reduce_start(cyc):
        rows = jnp.sum(jnp.sum(gacc[cyc], axis=1), axis=1, keepdims=True)
        ar1[cyc, gz] = jnp.sum(jnp.where(eye, rows, 0.0), axis=0, keepdims=True)
        for k in range(ngz - 1):
            line_copy(cyc, k).start()

    def reduce_middle(cyc):
        for k in range(ngz - 1):
            line_copy(cyc, k).wait_recv()
        ar2[cyc, gx * ngy + gy] = jnp.sum(ar1[cyc], axis=0)
        for k in range(ngx * ngy - 1):
            plane_copy(cyc, k).start()

    def reduce_end(cyc):
        for k in range(ngx * ngy - 1):
            plane_copy(cyc, k).wait_recv()
        total = jnp.sum(ar2[cyc], axis=0)
        rows = jnp.sum(jnp.where(eye, total, 0.0), axis=1, keepdims=True)
        gB[cyc] = jnp.broadcast_to(rows, (16, LANES))

    def solve(cyc):
        def G(i, j):
            i, j = min(i, j), max(i, j)
            return jnp.broadcast_to(gB[cyc, pl.ds(j * (j + 1) // 2 + i, 1), :], (8, LANES))

        g = [[G(i, j) for j in range(S + 1)] for i in range(S + 1)]
        gb = [[shifts[j] * g[i][j] + scale * g[i][j + 1] for j in range(S)] for i in range(S + 1)]
        h = [[shifts[i] * gb[i][j] + scale * gb[i + 1][j] if j <= i else None for j in range(S)] for i in range(S)]
        rhs = [gb[0][i] for i in range(S)]
        low = [[None] * S for _ in range(S)]
        dinv = [None] * S
        full = [[None] * S for _ in range(S)]
        for j in range(S):
            d = h[j][j]
            for k in range(j):
                d = d - low[j][k] * full[j][k]
            dinv[j] = 1.0 / d
            for i in range(j + 1, S):
                t = h[i][j]
                for k in range(j):
                    t = t - full[i][k] * low[j][k]
                full[i][j] = t
                low[i][j] = t * dinv[j]
        fwd = []
        for i in range(S):
            t = rhs[i]
            for k in range(i):
                t = t - low[i][k] * fwd[k]
            fwd.append(t)
        y = [None] * S
        for i in reversed(range(S)):
            t = fwd[i] * dinv[i]
            for k in range(i + 1, S):
                t = t - low[k][i] * y[k]
            y[i] = t
        c = []
        for j in range(S + 1):
            t = jnp.full((8, LANES), 1.0 if j == 0 else 0.0, jnp.float32)
            if j < S:
                t = t - shifts[j] * y[j]
            if j > 0:
                t = t - scale * y[j - 1]
            c.append(t)
        return y, c

    def put(n, value):
        cf[pl.ds(n, 1), :] = value[0:1]

    def coef(n):
        return cf[pl.ds(n, 1), :]

    for copy in loads[1:]:
        copy.wait()
    pack_edges(0)
    pl.semaphore_wait(barrier, 6)
    tell(0)
    send_edges(0)
    for lt in range(2):
        for side in range(2):
            send_x(0, side, lt)
        send_y(0, lt)
    loads[0].wait()

    def entry(p, e, x, lt):
        return st[p, e, x, :, lt * LANES:(lt + 1) * LANES].astype(jnp.float32) * inv

    for side in range(2):
        for e in range(4):
            for lt in range(2):
                edge = 0 if lt == 0 else LANES - 1
                xC[side, e, lt] = jnp.where(lane == edge, 0.0, entry(1 + side, e, 0 if side == 0 else NX - 1, lt))
                for x in range(NX):
                    part = st[3 + side, e, x, 16 * side:16 * side + 16, lt * LANES:(lt + 1) * LANES]
                    part = jnp.where(lane[:16] == edge, 0.0, part.astype(jnp.float32) * inv)
                    yC[side, e, lt, pl.ds(x, 1), :] = part[0:1] if side == 0 else part[15:16]
    for kind in range(2):
        ex, ey, ez = (jnp.zeros((8, LANES), jnp.float32),) * 3
        for side in range(2):
            for c in range(2):
                e = 3 * c if kind == 0 else c + 1
                for x in range(NX):
                    tile = entry(5 + side, e, x, side)
                    for t in range(4):
                        ez = place_edge(ez, tile, side, t, c, x)
                    ey = place_edge(ey, entry(3, e, x, side), side, 0, c, x)
                    ey = place_edge(ey, entry(4, e, x, side), side, 3, c, x)
                for p, x in ((1, 0), (2, NX - 1)):
                    tile = entry(p, e, x, side)
                    for t in range(4):
                        ex = place_edge(ex, tile, side, t, c, x)
        tile_y = (lane8 // 16) % 4
        inside = jnp.logical_or(
            jnp.logical_and(tile_y == 0, sub8 == 0), jnp.logical_and(tile_y == 3, sub8 == 7)
        )
        eC[0, kind] = ex
        eC[1, kind] = jnp.where(inside, ey, 0.0)
        eC[2, kind] = ez

    for j in range(S + AHEAD):
        interior(j, shifts[j % S])
        if j > 0:
            drain(j - 1)
        if j < 3:
            pl.semaphore_wait(near_sem.at[j], 6)
            if j < 2:
                tell(j + 1)
        if j < S:
            gram_row(0, 0, j)
        finish(j, True, False)
        if j + 1 == S:
            gram_row(0, 0, S)
            reduce_start(0)
        if j + 1 == S + 1:
            reduce_middle(0)
    if AHEAD == 0:
        reduce_middle(0)
    reduce_end(0)
    y, c = solve(0)
    for k in range(S):
        put(k, y[k])
    combo = [c + [None] * AHEAD]
    for j in range(AHEAD):
        old, new = combo[-1], []
        for k in range(NW):
            t = old[k - 1] if k > 0 else None
            factor = (shifts[k % S] - shifts[j]) * inv
            if old[k] is not None and factor != 0.0:
                t = factor * old[k] if t is None else t + factor * old[k]
            new.append(t)
        combo.append(new)
    place = {}
    for j in range(AHEAD + 1):
        for k in range(NW):
            if combo[j][k] is not None:
                place[j, k] = 8 + j * 8 + k
                put(place[j, k], combo[j][k])

    def combine(j, get, ks=range(NW)):
        t = None
        for k in ks:
            if (j, k) in place:
                term = coef(place[j, k]) * get(k)
                t = term if t is None else t + term
        return t

    def second(x, carry):
        for cc in range(2):
            for lt in range(2):
                rows = pl.ds(pl.multiple_of(row(x, lt), 8), NY)
                tiles = [W[k, cc, rows, :] for k in range(NW)]
                for j in range(AHEAD + 1):
                    W[NW + j, cc, rows, :] = combine(j, lambda k: tiles[k])
        return carry

    lax.fori_loop(1, NX + 1, second, 0)
    for j in range(AHEAD + 1):
        eb[NW + j] = combine(j, lambda k: eb[k])
    last = NW + AHEAD
    interior(last, shifts[AHEAD])
    for j in range(AHEAD + 1):
        gram_row(1, NW, j)
    drain(NW - 2)
    early = range(NW - 1)
    end = coef(place[AHEAD, NW - 1])
    for side in range(2):
        for cc in range(2):
            for lt in range(2):
                rows = pl.ds(row(0 if side == 0 else NX + 1, lt), NY)
                W[last, cc, rows, :] = combine(AHEAD, lambda k: W[k, cc, rows, :], early)
                yh[last, side, lt, cc] = combine(AHEAD, lambda k: yh[k, side, lt, cc], early)
    for d in range(6):
        eh[last, d] = combine(AHEAD, lambda k: eh[k, d], early)
    for side in range(2):
        for lt in range(2):
            wait_halo(y_copy(NW - 1, 1 - side, lt), side, 1)
            wait_halo(x_copy(NW - 1, 1 - side, lt), side, 0)
    for d in range(6):
        wait_edges(NW - 1, d)
        eh[last, d] = eh[last, d] + end * eh[NW - 1, d]
    for side in range(2):
        for cc in range(2):
            for lt in range(2):
                rows = pl.ds(row(0 if side == 0 else NX + 1, lt), NY)
                W[last, cc, rows, :] = W[last, cc, rows, :] + end * W[NW - 1, cc, rows, :]
                yh[last, side, lt, cc] = yh[last, side, lt, cc] + end * yh[NW - 1, side, lt, cc]
    edges_before = eb[last + 1]
    finish(last, False, True)

    gram_row(1, NW, S)
    edges = eb[last + 1]
    base = S * (S + 1) // 2
    for i in range(S):
        gacc[1, base + i] = gacc[1, base + i] + eb[NW + i] * (edges - edges_before)
    gacc[1, base + S] = gacc[1, base + S] + (edges * edges - edges_before * edges_before)
    reduce_start(1)
    unpack_edges(last + 1, range(NX))

    def first_share(x, carry):
        for cc in range(2):
            for lt in range(2):
                rows = pl.ds(pl.multiple_of(row(x, lt), 8), NY)
                t = coef(0) * W[0, cc, rows, :]
                for k in range(1, S):
                    t = t + coef(k) * W[k, cc, rows, :]
                lanes = slice(lt * LANES, (lt + 1) * LANES)
                first_ref[cc, x - 1, :, lanes] = t
                for k in range(S + 1):
                    basis_ref[k, cc, x - 1, :, lanes] = W[NW + k, cc, rows, :]
        return carry

    lax.fori_loop(1, NX + 1, first_share, 0)
    drain(NW - 1)
    for v in range(last + 1, NW + S):
        drain(v)
    for k in range(ngz - 1):
        line_copy(0, k).wait_send()
    for k in range(ngx * ngy - 1):
        plane_copy(0, k).wait_send()
    reduce_middle(1)
    for k in range(ngz - 1):
        line_copy(1, k).wait_send()
    reduce_end(1)
    y, c = solve(1)
    for k in range(S):
        weights_ref[k:k + 1, :] = y[k][0:1]
    for k in range(S + 1):
        weights_ref[8 + k:9 + k, :] = c[k][0:1]
    for k in range(ngx * ngy - 1):
        plane_copy(1, k).wait_send()


def store(first_ref, basis_ref, weights_ref, sol_hbm, res_hbm, sol, res, sem):
    copies = []
    for x in range(sol.shape[1]):
        for c in range(2):
            for lt in range(2):
                lanes = slice(lt * LANES, (lt + 1) * LANES)
                s, r = first_ref[c, x, :, lanes], None
                for k in range(S + 1):
                    tile = basis_ref[k, c, x, :, lanes]
                    if k < S:
                        s = s + weights_ref[k:k + 1, :] * tile
                    term = weights_ref[8 + k:9 + k, :] * tile
                    r = term if r is None else r + term
                sol[c, x, :, lanes] = s
                res[c, x, :, lanes] = r
        if x % 2 == 1:
            planes = pl.ds(x - 1, 2)
            for i, (src, dst) in enumerate(((sol, sol_hbm), (res, res_hbm))):
                copy = pltpu.make_async_copy(src.at[:, planes], dst.at[:, planes], sem.at[i, x // 2])
                copy.start()
                copies.append(copy)
    for copy in copies:
        copy.wait()


def solution(mesh):
    sizes = tuple(mesh.shape[a] for a in ("gx", "gy", "gz"))
    ngx, ngy, ngz = sizes

    def on_device(stencil, right_side):
        f32 = jnp.float32
        out = jax.ShapeDtypeStruct(right_side.shape, f32)
        dma = pltpu.SemaphoreType.DMA
        results = pl.pallas_call(
            functools.partial(kernel, sizes),
            out_shape=(
                out,
                jax.ShapeDtypeStruct((S + 1,) + right_side.shape, f32),
                jax.ShapeDtypeStruct((16, LANES), f32),
            ),
            in_specs=[pl.BlockSpec(memory_space=pl.ANY)] * 2,
            out_specs=(pl.BlockSpec(memory_space=pltpu.VMEM),) * 3,
            scratch_shapes=[
                pltpu.VMEM(stencil.shape, stencil.dtype),
                pltpu.VMEM((NV, 2, 20 * PITCH + 8, LANES), f32),
                pltpu.VMEM((2, 4, 2, 32, LANES), f32),
                pltpu.VMEM((2, 4, 2, 8, LANES), f32),
                pltpu.VMEM((3, 2, 8, LANES), f32),
                pltpu.VMEM((NV, 2, 2, 2, 8, LANES), f32),
                pltpu.VMEM((NV, 2, 2, 2, 8, LANES), f32),
                pltpu.VMEM((NV, 6, 8, LANES), f32),
                pltpu.VMEM((NV, 8, LANES), f32),
                pltpu.VMEM((2, 16, 8, LANES), f32),
                pltpu.VMEM((2, ngz, 1, LANES), f32),
                pltpu.VMEM((2, ngx * ngy, 1, LANES), f32),
                pltpu.VMEM((2, 16, LANES), f32),
                pltpu.VMEM((40, LANES), f32),
                dma((17,)),
                pltpu.SemaphoreType.REGULAR((3,)),
                dma((NV, 14)),
                dma((NV, 14)),
                dma((2, ngz - 1)),
                dma((2, ngz - 1)),
                dma((2, ngx * ngy - 1)),
                dma((2, ngx * ngy - 1)),
            ],
            compiler_params=pltpu.CompilerParams(
                collective_id=0, has_side_effects=True, vmem_limit_bytes=48 << 20
            ),
            name="gmres",
        )(
            pltpu.with_memory_space_constraint(stencil, pltpu.HBM),
            pltpu.with_memory_space_constraint(right_side, pltpu.HBM),
        )
        results = [pltpu.with_memory_space_constraint(r, pltpu.VMEM) for r in results]
        return pl.pallas_call(
            store,
            out_shape=(out, out),
            in_specs=[pl.BlockSpec(memory_space=pltpu.VMEM)] * 3,
            out_specs=(pl.BlockSpec(memory_space=pl.ANY),) * 2,
            scratch_shapes=[
                pltpu.VMEM(right_side.shape, f32),
                pltpu.VMEM(right_side.shape, f32),
                dma((2, right_side.shape[1] // 2)),
            ],
            compiler_params=pltpu.CompilerParams(vmem_limit_bytes=4 << 20),
            name="store",
        )(*results)

    specs = (P(None, None, "gx", "gy", "gz"), P(None, "gx", "gy", "gz"))
    return jax.shard_map(
        on_device, mesh=mesh, in_specs=specs, out_specs=(specs[1], specs[1]), check_vma=False
    )
```

```python
import functools

import jax
import jax.numpy as jnp
from jax import lax
from jax.experimental import pallas as pl
from jax.experimental.pallas import tpu as pltpu
from jax.sharding import PartitionSpec as P

MESH = pl.DeviceIdType.MESH
S = 4
AHEAD = S - 1
shifts = (15.0, 2.0, 8.5, 4.75)
scale = 6.5
inv = 1.0 / scale

NW = S + 1 + AHEAD
NV = NW + S + 1
PITCH = 40
LANES = 128


def row(x, lt):
    return (2 * x + lt) * PITCH + 8


def kernel(
    sizes, st_hbm, rs_hbm, first_ref, basis_ref, weights_ref,
    st, W, xC, yC, eC, yh, ys, eh, eb, gacc, ar1, ar2, pair, chips, gB, cf,
    load_sem, near_sem, ssem, rsem, s1sem, r1sem, s2sem, r2sem, pair_sem, s3sem, r3sem,
):
    ngx, ngy, ngz = sizes
    gx, gy, gz = (lax.axis_index(a) for a in ("gx", "gy", "gz"))
    NX, NY = 8, 32
    have = (gx > 0, gx < ngx - 1, gy > 0, gy < ngy - 1, gz > 0, gz < ngz - 1)
    beside = (
        {"gx": lax.rem(gx + ngx - 1, ngx)}, {"gx": lax.rem(gx + 1, ngx)},
        {"gy": lax.rem(gy + ngy - 1, ngy)}, {"gy": lax.rem(gy + 1, ngy)},
        {"gz": lax.rem(gz + ngz - 1, ngz)}, {"gz": lax.rem(gz + 1, ngz)},
    )
    line = [{"gz": lax.rem(gz + k, ngz)} for k in range(1, ngz)]
    plane = [
        {"gx": lax.rem(gx + k // ngy, ngx), "gy": lax.rem(gy + k % ngy, ngy)}
        for k in range(1, ngx * ngy)
    ]
    lane = lax.broadcasted_iota(jnp.int32, (NY, LANES), 1)
    lane8 = lax.broadcasted_iota(jnp.int32, (8, LANES), 1)
    sub8 = lax.broadcasted_iota(jnp.int32, (8, LANES), 0)
    eye = lax.broadcasted_iota(jnp.int32, (16, LANES), 1) == lax.broadcasted_iota(jnp.int32, (16, LANES), 0)
    zero = jnp.zeros((NY, LANES), jnp.float32)

    loads = [pltpu.make_async_copy(st_hbm, st, load_sem.at[0])]
    for lt in range(2):
        for x in range(NX):
            loads.append(
                pltpu.make_async_copy(
                    rs_hbm.at[:, x, :, pl.ds(lt * LANES, LANES)],
                    W.at[0, :, pl.ds(row(x + 1, lt), NY), :],
                    load_sem.at[1 + lt * NX + x],
                )
            )
    for copy in loads[1:]:
        copy.start()
    loads[0].start()

    barrier = pltpu.get_barrier_semaphore()
    for peer in beside:
        pl.semaphore_signal(barrier, inc=1, device_id=peer, device_id_type=MESH)

    for v in range(NV):
        for c in range(2):
            for x in range(1, NX + 1):
                for lt in range(2):
                    W[v, c, pl.ds(row(x, lt) - 8, 8), :] = jnp.zeros((8, LANES), jnp.float32)
            W[v, c, pl.ds(row(NX + 1, 0) - 8, 8), :] = jnp.zeros((8, LANES), jnp.float32)
    for d in range(2):
        @pl.when(jnp.logical_not(have[d]))
        def _():
            for v in range(NV):
                for c in range(2):
                    for lt in range(2):
                        W[v, c, pl.ds(row(0 if d == 0 else NX + 1, lt), NY), :] = zero

        @pl.when(jnp.logical_not(have[2 + d]))
        def _():
            for v in range(NV):
                yh[v, d] = jnp.zeros((2, 2, NX, LANES), jnp.float32)

    for d in range(6):
        @pl.when(jnp.logical_not(have[d]))
        def _():
            for v in range(NV):
                eh[v, d] = jnp.zeros((8, LANES), jnp.float32)

    for cyc in range(2):
        gacc[cyc, 15] = jnp.zeros((8, LANES), jnp.float32)

    def tell(step):
        for peer in beside:
            pl.semaphore_signal(near_sem.at[step], inc=1, device_id=peer, device_id_type=MESH)

    def x_copy(v, side, lt):
        src = W.at[v, :, pl.ds(row(1 if side == 0 else NX, lt), NY), :]
        dst = W.at[v, :, pl.ds(row(NX + 1 if side == 0 else 0, lt), NY), :]
        k = 2 * side + lt
        return pltpu.make_async_remote_copy(
            src, dst, ssem.at[v, k], rsem.at[v, k], device_id=beside[side], device_id_type=MESH
        )

    def y_copy(v, side, lt):
        k = 10 + 2 * side + lt
        return pltpu.make_async_remote_copy(
            ys.at[v, side, lt], yh.at[v, 1 - side, lt], ssem.at[v, k], rsem.at[v, k],
            device_id=beside[2 + side], device_id_type=MESH,
        )

    def e_copy(v, d):
        return pltpu.make_async_remote_copy(
            eb.at[v], eh.at[v, d ^ 1], ssem.at[v, 4 + d], rsem.at[v, 4 + d],
            device_id=beside[d], device_id_type=MESH,
        )

    def send_x(v, side, lt):
        @pl.when(have[side])
        def _():
            x_copy(v, side, lt).start()

    def send_y(v, lt):
        for side in range(2):
            @pl.when(have[2 + side])
            def _():
                for c in range(2):
                    ys[v, side, lt, c] = W[
                        v, c, pl.ds(row(1, lt) + (0 if side == 0 else NY - 1), NX, stride=2 * PITCH), :
                    ]
                y_copy(v, side, lt).start()

    def send_edges(v):
        for d in range(6):
            @pl.when(have[d])
            def _():
                e_copy(v, d).start()

    def place_edge(packed, tile, side, t, c, x):
        n = side * 64 + t * 16 + c * 8 + x
        turn = n if side == 0 else (n + 1) % LANES
        tile = tile[8 * t:8 * t + 8]
        if turn:
            tile = pltpu.roll(tile, turn, 1)
        return jnp.where(lane8 == n, tile, packed)

    def pack_edges(v):
        packed = jnp.zeros((8, LANES), jnp.float32)
        for side in range(2):
            for c in range(2):
                for x in range(NX):
                    tile = W[v, c, pl.ds(row(x + 1, side), NY), :]
                    for t in range(4):
                        packed = place_edge(packed, tile, side, t, c, x)
        eb[v] = packed

    def unpack_edges(v, planes):
        packed = eb[v]
        for side in range(2):
            edge = 0 if side == 0 else LANES - 1
            for c in range(2):
                for x in planes:
                    for t in range(4):
                        turn = (edge - (side * 64 + t * 16 + c * 8 + x)) % LANES
                        moved = pltpu.roll(packed, turn, 1) if turn else packed
                        rows = pl.ds(row(x + 1, side) + 8 * t, 8)
                        W[v, c, rows, :] = jnp.where(lane8 == edge, moved, W[v, c, rows, :])

    def swapped(h):
        return jnp.where((lane8 & 8) == 0, pltpu.roll(h, LANES - 8, 1), pltpu.roll(h, 8, 1))

    def fix_edges(v):
        hz = pltpu.roll(jnp.where(lane8 < 64, eh[v, 5], eh[v, 4]), 64, 1)
        hy = jnp.where(
            sub8 == 0,
            pltpu.roll(pltpu.roll(eh[v, 2], LANES - 48, 1), 1, 0),
            pltpu.roll(pltpu.roll(eh[v, 3], 48, 1), 7, 0),
        )
        hx = jnp.where((lane8 & 7) == 0, pltpu.roll(eh[v, 0], LANES - 7, 1), pltpu.roll(eh[v, 1], 7, 1))
        part = eb[v + 1]
        for axis, h in enumerate((hx, hy, hz)):
            part = part + (eC[axis, 0] * h + eC[axis, 1] * swapped(h))
        eb[v + 1] = part

    def wait_halo(copy, side, axis):
        @pl.when(have[2 * axis + side])
        def _():
            copy.wait_recv()

    def wait_edges(v, d):
        @pl.when(have[d])
        def _():
            e_copy(v, d ^ 1).wait_recv()

    def interior_plane(v, x, left, right, shift):
        out = v + 1
        acc = [[None, None], [None, None]]

        def add(lt, p, b, src):
            for a in range(2):
                term = st[p, 2 * a + b, x - 1, :, lt * LANES:(lt + 1) * LANES].astype(jnp.float32) * src
                acc[lt][a] = term if acc[lt][a] is None else acc[lt][a] + term

        def at(b, xx, lt, off=0):
            start = row(xx, lt)
            if off == 0 and not isinstance(start, int):
                start = pl.multiple_of(start, 8)
            return W[v, b, pl.ds(start + off, NY), :]

        for b in range(2):
            centre = [at(b, x, lt) for lt in range(2)]
            up = [pltpu.roll(t, 1, 1) for t in centre]
            down = [pltpu.roll(t, LANES - 1, 1) for t in centre]
            for lt in range(2):
                add(lt, 0, b, centre[lt])
            add(0, 5, b, jnp.where(lane == 0, 0.0, up[0]))
            add(1, 5, b, jnp.where(lane == 0, up[0], up[1]))
            add(0, 6, b, jnp.where(lane == LANES - 1, down[1], down[0]))
            add(1, 6, b, jnp.where(lane == LANES - 1, 0.0, down[1]))
            for lt in range(2):
                if left:
                    add(lt, 1, b, at(b, x - 1, lt))
                if right:
                    add(lt, 2, b, at(b, x + 1, lt))
                add(lt, 3, b, at(b, x, lt, -1))
                add(lt, 4, b, at(b, x, lt, 1))
        for lt in range(2):
            for a in range(2):
                start = row(x, lt)
                if not isinstance(start, int):
                    start = pl.multiple_of(start, 8)
                W[out, a, pl.ds(start, NY), :] = (acc[lt][a] - shift * at(a, x, lt)) * inv

    def interior(v, shift):
        interior_plane(v, 1, False, True, shift)

        def body(x, carry):
            interior_plane(v, x, True, True, shift)
            return carry

        lax.fori_loop(2, NX, body, 0)
        interior_plane(v, NX, True, False, shift)
        pack_edges(v + 1)

    def fix_y(v, side, lt):
        out = v + 1
        h = [yh[v, side, lt, b] for b in range(2)]
        for a in range(2):
            part = yC[side, 2 * a, lt] * h[0] + yC[side, 2 * a + 1, lt] * h[1]
            rows = pl.ds(row(1, lt) + (0 if side == 0 else NY - 1), NX, stride=2 * PITCH)
            W[out, a, rows, :] = W[out, a, rows, :] + part

    def fix_x(v, side, lt):
        out = v + 1
        src = row(0 if side == 0 else NX + 1, lt)
        dst = pl.ds(row(1 if side == 0 else NX, lt), NY)
        h = [W[v, b, pl.ds(src, NY), :] for b in range(2)]
        for a in range(2):
            part = xC[side, 2 * a, lt] * h[0] + xC[side, 2 * a + 1, lt] * h[1]
            W[out, a, dst, :] = W[out, a, dst, :] + part

    def finish(v, sent, local):
        if not local:
            for d in range(6):
                wait_edges(v, d)
        fix_edges(v)
        if sent:
            send_edges(v + 1)
        if sent:
            unpack_edges(v + 1, (0, NX - 1))
        for lt in range(2):
            for side in range(2):
                @pl.when(have[2 + side])
                def _():
                    if not local:
                        y_copy(v, 1 - side, lt).wait_recv()
                    fix_y(v, side, lt)

            for side in range(2):
                @pl.when(have[side])
                def _():
                    if not local:
                        x_copy(v, 1 - side, lt).wait_recv()
                    fix_x(v, side, lt)
                    if sent:
                        x_copy(v + 1, side, lt).start()
            if sent:
                send_y(v + 1, lt)
        if sent:
            unpack_edges(v + 1, range(1, NX - 1))

    def drain(v):
        for d in range(6):
            @pl.when(have[d])
            def _():
                if d < 2:
                    for lt in range(2):
                        x_copy(v, d, lt).wait_send()
                elif d < 4:
                    for lt in range(2):
                        y_copy(v, d - 2, lt).wait_send()
                e_copy(v, d).wait_send()

    def gram_row(cyc, first, j):
        def body(x, accs):
            accs = list(accs)
            for c in range(2):
                for lt in range(2):
                    rows = pl.ds(pl.multiple_of(row(x, lt), 8), NY)
                    right = W[first + j, c, rows, :]
                    for i in range(j + 1):
                        left = right if i == j else W[first + i, c, rows, :]
                        accs[i] = accs[i] + jnp.sum((left * right).reshape(NY // 8, 8, LANES), axis=0)
            return tuple(accs)

        accs = lax.fori_loop(1, NX + 1, body, tuple(jnp.zeros((8, LANES), jnp.float32) for _ in range(j + 1)))
        for i in range(j + 1):
            gacc[cyc, j * (j + 1) // 2 + i] = accs[i]

    def line_copy(k):
        return pltpu.make_async_remote_copy(
            ar1.at[gz], ar1.at[gz], s1sem.at[k], r1sem.at[k], device_id=line[k], device_id_type=MESH
        )

    def plane_copy(k):
        slot = gx * ngy + gy
        return pltpu.make_async_remote_copy(
            ar2.at[slot], ar2.at[slot], s2sem.at[k], r2sem.at[k], device_id=plane[k], device_id_type=MESH
        )

    core = lax.rem(gz, 2)
    nchip = ngz // 2
    far = []
    for k in range(1, ngx * ngy * nchip):
        i, j, m = k // (ngy * nchip), k // nchip % ngy, k % nchip
        far.append((-min(i, ngx - i) - min(j, ngy - j) - min(m, nchip - m), i, j, m))
    far.sort()

    def pair_copy():
        return pltpu.make_async_remote_copy(
            pair.at[core], pair.at[core], pair_sem.at[0], pair_sem.at[1],
            device_id={"gz": gz + 1 - 2 * core}, device_id_type=MESH,
        )

    def chip_copy(k):
        _, i, j, m = far[k]
        slot = (gx * ngy + gy) * nchip + lax.div(gz, 2)
        peer = {"gx": lax.rem(gx + i, ngx), "gy": lax.rem(gy + j, ngy), "gz": lax.rem(gz + 2 * m, ngz)}
        return pltpu.make_async_remote_copy(
            chips.at[slot], chips.at[slot], s3sem.at[k], r3sem.at[k], device_id=peer, device_id_type=MESH
        )

    def own_sums(cyc):
        rows = jnp.sum(jnp.sum(gacc[cyc], axis=1), axis=1, keepdims=True)
        return jnp.sum(jnp.where(eye, rows, 0.0), axis=0, keepdims=True)

    def spread(cyc, total):
        rows = jnp.sum(jnp.where(eye, total, 0.0), axis=1, keepdims=True)
        gB[cyc] = jnp.broadcast_to(rows, (16, LANES))

    def reduce_start(cyc):
        if cyc == 0:
            ar1[gz] = own_sums(0)
            for k in range(ngz - 1):
                line_copy(k).start()
        else:
            pair[core] = own_sums(1)
            pair_copy().start()

    def reduce_middle(cyc):
        if cyc == 0:
            for k in range(ngz - 1):
                line_copy(k).wait_recv()
            ar2[gx * ngy + gy] = jnp.sum(ar1[...], axis=0)
            for k in range(ngx * ngy - 1):
                plane_copy(k).start()
        else:
            pair_copy().wait_recv()
            chips[(gx * ngy + gy) * nchip + lax.div(gz, 2)] = pair[0] + pair[1]
            for k in range(len(far)):
                chip_copy(k).start()

    def reduce_end(cyc):
        if cyc == 0:
            for k in range(ngx * ngy - 1):
                plane_copy(k).wait_recv()
            spread(0, jnp.sum(ar2[...], axis=0))
        else:
            for k in range(len(far)):
                chip_copy(k).wait_recv()
            spread(1, jnp.sum(chips[...], axis=0))

    def reduce_drain(cyc):
        if cyc == 0:
            for k in range(ngz - 1):
                line_copy(k).wait_send()
            for k in range(ngx * ngy - 1):
                plane_copy(k).wait_send()
        else:
            pair_copy().wait_send()
            for k in range(len(far)):
                chip_copy(k).wait_send()

    def solve(cyc):
        def G(i, j):
            i, j = min(i, j), max(i, j)
            return jnp.broadcast_to(gB[cyc, pl.ds(j * (j + 1) // 2 + i, 1), :], (8, LANES))

        g = [[G(i, j) for j in range(S + 1)] for i in range(S + 1)]
        gb = [[shifts[j] * g[i][j] + scale * g[i][j + 1] for j in range(S)] for i in range(S + 1)]
        h = [[shifts[i] * gb[i][j] + scale * gb[i + 1][j] if j <= i else None for j in range(S)] for i in range(S)]
        rhs = [gb[0][i] for i in range(S)]
        low = [[None] * S for _ in range(S)]
        dinv = [None] * S
        full = [[None] * S for _ in range(S)]
        for j in range(S):
            d = h[j][j]
            for k in range(j):
                d = d - low[j][k] * full[j][k]
            dinv[j] = 1.0 / d
            for i in range(j + 1, S):
                t = h[i][j]
                for k in range(j):
                    t = t - full[i][k] * low[j][k]
                full[i][j] = t
                low[i][j] = t * dinv[j]
        fwd = []
        for i in range(S):
            t = rhs[i]
            for k in range(i):
                t = t - low[i][k] * fwd[k]
            fwd.append(t)
        y = [None] * S
        for i in reversed(range(S)):
            t = fwd[i] * dinv[i]
            for k in range(i + 1, S):
                t = t - low[k][i] * y[k]
            y[i] = t
        c = []
        for j in range(S + 1):
            t = jnp.full((8, LANES), 1.0 if j == 0 else 0.0, jnp.float32)
            if j < S:
                t = t - shifts[j] * y[j]
            if j > 0:
                t = t - scale * y[j - 1]
            c.append(t)
        return y, c

    def put(n, value):
        cf[pl.ds(n, 1), :] = value[0:1]

    def coef(n):
        return cf[pl.ds(n, 1), :]

    for copy in loads[1:]:
        copy.wait()
    pack_edges(0)
    pl.semaphore_wait(barrier, 6)
    tell(0)
    send_edges(0)
    for lt in range(2):
        for side in range(2):
            send_x(0, side, lt)
        send_y(0, lt)
    loads[0].wait()

    def entry(p, e, x, lt):
        return st[p, e, x, :, lt * LANES:(lt + 1) * LANES].astype(jnp.float32) * inv

    for side in range(2):
        for e in range(4):
            for lt in range(2):
                edge = 0 if lt == 0 else LANES - 1
                xC[side, e, lt] = jnp.where(lane == edge, 0.0, entry(1 + side, e, 0 if side == 0 else NX - 1, lt))
                for x in range(NX):
                    part = st[3 + side, e, x, 16 * side:16 * side + 16, lt * LANES:(lt + 1) * LANES]
                    part = jnp.where(lane[:16] == edge, 0.0, part.astype(jnp.float32) * inv)
                    yC[side, e, lt, pl.ds(x, 1), :] = part[0:1] if side == 0 else part[15:16]
    for kind in range(2):
        ex, ey, ez = (jnp.zeros((8, LANES), jnp.float32),) * 3
        for side in range(2):
            for c in range(2):
                e = 3 * c if kind == 0 else c + 1
                for x in range(NX):
                    tile = entry(5 + side, e, x, side)
                    for t in range(4):
                        ez = place_edge(ez, tile, side, t, c, x)
                    ey = place_edge(ey, entry(3, e, x, side), side, 0, c, x)
                    ey = place_edge(ey, entry(4, e, x, side), side, 3, c, x)
                for p, x in ((1, 0), (2, NX - 1)):
                    tile = entry(p, e, x, side)
                    for t in range(4):
                        ex = place_edge(ex, tile, side, t, c, x)
        tile_y = (lane8 // 16) % 4
        inside = jnp.logical_or(
            jnp.logical_and(tile_y == 0, sub8 == 0), jnp.logical_and(tile_y == 3, sub8 == 7)
        )
        eC[0, kind] = ex
        eC[1, kind] = jnp.where(inside, ey, 0.0)
        eC[2, kind] = ez

    for j in range(S + AHEAD):
        interior(j, shifts[j % S])
        if j > 0:
            drain(j - 1)
        if j < 3:
            pl.semaphore_wait(near_sem.at[j], 6)
            if j < 2:
                tell(j + 1)
        if j < S:
            gram_row(0, 0, j)
        finish(j, True, False)
        if j + 1 == S:
            gram_row(0, 0, S)
            reduce_start(0)
        if j + 1 == S + 1:
            reduce_middle(0)
    if AHEAD == 0:
        reduce_middle(0)
    reduce_end(0)
    y, c = solve(0)
    for k in range(S):
        put(k, y[k])
    combo = [c + [None] * AHEAD]
    for j in range(AHEAD):
        old, new = combo[-1], []
        for k in range(NW):
            t = old[k - 1] if k > 0 else None
            factor = (shifts[k % S] - shifts[j]) * inv
            if old[k] is not None and factor != 0.0:
                t = factor * old[k] if t is None else t + factor * old[k]
            new.append(t)
        combo.append(new)
    place = {}
    for j in range(AHEAD + 1):
        for k in range(NW):
            if combo[j][k] is not None:
                place[j, k] = 8 + j * 8 + k
                put(place[j, k], combo[j][k])

    def combine(j, get, ks=range(NW)):
        t = None
        for k in ks:
            if (j, k) in place:
                term = coef(place[j, k]) * get(k)
                t = term if t is None else t + term
        return t

    def second(x, carry):
        for cc in range(2):
            for lt in range(2):
                rows = pl.ds(pl.multiple_of(row(x, lt), 8), NY)
                tiles = [W[k, cc, rows, :] for k in range(NW)]
                for j in range(AHEAD + 1):
                    W[NW + j, cc, rows, :] = combine(j, lambda k: tiles[k])
        return carry

    lax.fori_loop(1, NX + 1, second, 0)
    for j in range(AHEAD + 1):
        eb[NW + j] = combine(j, lambda k: eb[k])
    last = NW + AHEAD
    interior(last, shifts[AHEAD])
    for j in range(AHEAD + 1):
        gram_row(1, NW, j)
    drain(NW - 2)
    early = range(NW - 1)
    end = coef(place[AHEAD, NW - 1])
    for side in range(2):
        for cc in range(2):
            for lt in range(2):
                rows = pl.ds(row(0 if side == 0 else NX + 1, lt), NY)
                W[last, cc, rows, :] = combine(AHEAD, lambda k: W[k, cc, rows, :], early)
                yh[last, side, lt, cc] = combine(AHEAD, lambda k: yh[k, side, lt, cc], early)
    for d in range(6):
        eh[last, d] = combine(AHEAD, lambda k: eh[k, d], early)
    for side in range(2):
        for lt in range(2):
            wait_halo(y_copy(NW - 1, 1 - side, lt), side, 1)
            wait_halo(x_copy(NW - 1, 1 - side, lt), side, 0)
    for d in range(6):
        wait_edges(NW - 1, d)
        eh[last, d] = eh[last, d] + end * eh[NW - 1, d]
    for side in range(2):
        for cc in range(2):
            for lt in range(2):
                rows = pl.ds(row(0 if side == 0 else NX + 1, lt), NY)
                W[last, cc, rows, :] = W[last, cc, rows, :] + end * W[NW - 1, cc, rows, :]
                yh[last, side, lt, cc] = yh[last, side, lt, cc] + end * yh[NW - 1, side, lt, cc]
    edges_before = eb[last + 1]
    finish(last, False, True)

    gram_row(1, NW, S)
    edges = eb[last + 1]
    base = S * (S + 1) // 2
    for i in range(S):
        gacc[1, base + i] = gacc[1, base + i] + eb[NW + i] * (edges - edges_before)
    gacc[1, base + S] = gacc[1, base + S] + (edges * edges - edges_before * edges_before)
    reduce_start(1)
    reduce_middle(1)
    unpack_edges(last + 1, range(NX))

    def first_share(x, carry):
        for cc in range(2):
            for lt in range(2):
                rows = pl.ds(pl.multiple_of(row(x, lt), 8), NY)
                t = coef(0) * W[0, cc, rows, :]
                for k in range(1, S):
                    t = t + coef(k) * W[k, cc, rows, :]
                lanes = slice(lt * LANES, (lt + 1) * LANES)
                first_ref[cc, x - 1, :, lanes] = t
                for k in range(S + 1):
                    basis_ref[k, cc, x - 1, :, lanes] = W[NW + k, cc, rows, :]
        return carry

    lax.fori_loop(1, NX + 1, first_share, 0)
    drain(NW - 1)
    for v in range(last + 1, NW + S):
        drain(v)
    reduce_drain(0)
    reduce_end(1)
    y, c = solve(1)
    for k in range(S):
        weights_ref[k:k + 1, :] = y[k][0:1]
    for k in range(S + 1):
        weights_ref[8 + k:9 + k, :] = c[k][0:1]
    reduce_drain(1)


def store(first_ref, basis_ref, weights_ref, sol_hbm, res_hbm, sol, res, sem):
    copies = []
    for x in range(sol.shape[1]):
        for c in range(2):
            for lt in range(2):
                lanes = slice(lt * LANES, (lt + 1) * LANES)
                s, r = first_ref[c, x, :, lanes], None
                for k in range(S + 1):
                    tile = basis_ref[k, c, x, :, lanes]
                    if k < S:
                        s = s + weights_ref[k:k + 1, :] * tile
                    term = weights_ref[8 + k:9 + k, :] * tile
                    r = term if r is None else r + term
                sol[c, x, :, lanes] = s
                res[c, x, :, lanes] = r
        if x % 2 == 1:
            planes = pl.ds(x - 1, 2)
            for i, (src, dst) in enumerate(((sol, sol_hbm), (res, res_hbm))):
                copy = pltpu.make_async_copy(src.at[:, planes], dst.at[:, planes], sem.at[i, x // 2])
                copy.start()
                copies.append(copy)
    for copy in copies:
        copy.wait()


def solution(mesh):
    sizes = tuple(mesh.shape[a] for a in ("gx", "gy", "gz"))
    ngx, ngy, ngz = sizes

    def on_device(stencil, right_side):
        f32 = jnp.float32
        out = jax.ShapeDtypeStruct(right_side.shape, f32)
        dma = pltpu.SemaphoreType.DMA
        results = pl.pallas_call(
            functools.partial(kernel, sizes),
            out_shape=(
                out,
                jax.ShapeDtypeStruct((S + 1,) + right_side.shape, f32),
                jax.ShapeDtypeStruct((16, LANES), f32),
            ),
            in_specs=[pl.BlockSpec(memory_space=pl.ANY)] * 2,
            out_specs=(pl.BlockSpec(memory_space=pltpu.VMEM),) * 3,
            scratch_shapes=[
                pltpu.VMEM(stencil.shape, stencil.dtype),
                pltpu.VMEM((NV, 2, 20 * PITCH + 8, LANES), f32),
                pltpu.VMEM((2, 4, 2, 32, LANES), f32),
                pltpu.VMEM((2, 4, 2, 8, LANES), f32),
                pltpu.VMEM((3, 2, 8, LANES), f32),
                pltpu.VMEM((NV, 2, 2, 2, 8, LANES), f32),
                pltpu.VMEM((NV, 2, 2, 2, 8, LANES), f32),
                pltpu.VMEM((NV, 6, 8, LANES), f32),
                pltpu.VMEM((NV, 8, LANES), f32),
                pltpu.VMEM((2, 16, 8, LANES), f32),
                pltpu.VMEM((ngz, 1, LANES), f32),
                pltpu.VMEM((ngx * ngy, 1, LANES), f32),
                pltpu.VMEM((2, 1, LANES), f32),
                pltpu.VMEM((ngx * ngy * ngz // 2, 1, LANES), f32),
                pltpu.VMEM((2, 16, LANES), f32),
                pltpu.VMEM((40, LANES), f32),
                dma((17,)),
                pltpu.SemaphoreType.REGULAR((3,)),
                dma((NV, 14)),
                dma((NV, 14)),
                dma((ngz - 1,)),
                dma((ngz - 1,)),
                dma((ngx * ngy - 1,)),
                dma((ngx * ngy - 1,)),
                dma((2,)),
                dma((ngx * ngy * ngz // 2 - 1,)),
                dma((ngx * ngy * ngz // 2 - 1,)),
            ],
            compiler_params=pltpu.CompilerParams(
                collective_id=0, has_side_effects=True, vmem_limit_bytes=48 << 20
            ),
            name="gmres",
        )(
            pltpu.with_memory_space_constraint(stencil, pltpu.HBM),
            pltpu.with_memory_space_constraint(right_side, pltpu.HBM),
        )
        results = [pltpu.with_memory_space_constraint(r, pltpu.VMEM) for r in results]
        return pl.pallas_call(
            store,
            out_shape=(out, out),
            in_specs=[pl.BlockSpec(memory_space=pltpu.VMEM)] * 3,
            out_specs=(pl.BlockSpec(memory_space=pl.ANY),) * 2,
            scratch_shapes=[
                pltpu.VMEM(right_side.shape, f32),
                pltpu.VMEM(right_side.shape, f32),
                dma((2, right_side.shape[1] // 2)),
            ],
            compiler_params=pltpu.CompilerParams(vmem_limit_bytes=4 << 20),
            name="store",
        )(*results)

    specs = (P(None, None, "gx", "gy", "gz"), P(None, "gx", "gy", "gz"))
    return jax.shard_map(
        on_device, mesh=mesh, in_specs=specs, out_specs=(specs[1], specs[1]), check_vma=False
    )
```
